32 devices in a mesh: row: 4 (over y, x), col: 8 (over z, core).
Axes of the slice: x: 2, y: 2, z: 4, core: 2. Of those that a mesh axis runs over, the one named last changes fastest.
Arguments:
- features: bfloat16 [64, 512, 512], P(None, 'col', 'row'), may hold values from -120 to 120
- conv_first: bfloat16 [9, 64, 64], replicated, may hold values from -0.25 to 0.25
- conv_second: bfloat16 [9, 64, 64], replicated, may hold values from -0.25 to 0.25
- head_weight: bfloat16 [37, 64], replicated, may hold values from -0.75 to 0.75
- head_bias: float32 [37], replicated, may hold values from -4 to 4
- cotangent: bfloat16 [37, 512, 512], P(None, 'col', 'row'), may hold values from -6 to 6
Outputs:
- logits: bfloat16 [37, 512, 512], P(None, 'col', 'row')
- input_grad: bfloat16 [64, 512, 512], P(None, 'col', 'row')
- grad_first: float32 [9, 64, 64], replicated
- grad_second: float32 [9, 64, 64], replicated
- grad_head: float32 [37, 64], replicated
- grad_bias: float32 [37], replicated
The draws below stay inside these ranges and needn't reach their ends.
All inputs are finite; a program needn't handle non-finite values.
Results may differ from the reference program's by a relative error of at most 0.007.
Values may be sent and summed in bfloat16 or wider, within the bound.
A program may use at most 128 MiB of HBM per device.

```python
import jax
import jax.numpy as jnp
from jax import lax

C = 64
NB = 37
DILATION_STEP = 16
L = 512


def draw_features(key, part):
    subkeys = jax.random.split(key, 3)
    position = jnp.arange(L, dtype=jnp.float32) / L
    row_scale = jnp.exp(jax.random.uniform(subkeys[1], (L,), minval=-1.15, maxval=1.15) + 0.55 * (2.0 * position - 1.0))
    col_scale = jnp.exp(jax.random.uniform(subkeys[2], (L,), minval=-1.15, maxval=1.15) + 0.3 * (2.0 * position - 1.0))
    baseline = jax.random.normal(subkeys[0], (C, L, L))
    baseline = jnp.clip(baseline, -5.0, 5.0)
    return (baseline * col_scale[None, :, None] * row_scale[None, None, :]).astype(jnp.bfloat16)


def block_scale(key, dims, shards, least, largest):
    def one(dim, blocks):
        steps = jax.random.uniform(jax.random.fold_in(jax.random.fold_in(key, 6), dim), (blocks,), jnp.float32, least / len(shards), largest / len(shards))
        return jnp.repeat(jnp.exp(steps), dims[dim] // blocks).reshape((-1,) + (1,) * (len(dims) - dim - 1))

    gain = one(*shards[0])
    for cut in shards[1:]:
        gain = gain * one(*cut)
    return gain


def scatter_about(stream_key, shape, scale, most, cuts=(), held_as=jnp.bfloat16):
    gain = block_scale(stream_key, shape, cuts, -0.22, 0.18) if cuts else 1.0
    array = jax.random.normal(stream_key, shape, jnp.float32) * scale * gain
    return jnp.minimum(jnp.maximum(array, -most), most).astype(held_as)


def setup_inputs(seed: int = 0) -> dict:
    key_of = jax.random.split(jax.random.key(seed), 7)
    return {
        "features": draw_features(jax.random.fold_in(key_of[6], 71), 0),
        "conv_first": scatter_about(key_of[1], (9, C, C), (9 * C) ** -0.5, 0.25),
        "conv_second": scatter_about(key_of[2], (9, C, C), (9 * C) ** -0.5, 0.25),
        "head_weight": scatter_about(key_of[3], (NB, C), C ** -0.5, 0.75),
        "head_bias": scatter_about(key_of[4], (NB,), 1.0, 4.0, (), jnp.float32),
        "cotangent": scatter_about(key_of[5], (NB, L, L), 1.0, 6.0, ((1, 8), (2, 4))),
    }


epsilon = 1e-05

def elu_apply(value_entries):
    return jnp.where(value_entries > 0, value_entries, jnp.exp(jnp.minimum(value_entries, 0.0)) - 1.0)

def elu_slope(value_entries):
    return jnp.where(value_entries > 0, 1.0, jnp.exp(jnp.minimum(value_entries, 0.0)))

def widen(value_entries):
    return jnp.pad(value_entries, ((0, 0), (DILATION_STEP, DILATION_STEP), (DILATION_STEP, DILATION_STEP)))

def tap_window(padded, kernel_row, kernel_column, adjoint, col_count, row_count):
    shift_direction = -1 if adjoint else 1
    column_shift = DILATION_STEP + shift_direction * DILATION_STEP * (kernel_column - 1)
    row_shift = DILATION_STEP + shift_direction * DILATION_STEP * (kernel_row - 1)
    window = padded[:, column_shift:column_shift + col_count, row_shift:row_shift + row_count]
    return window.reshape(padded.shape[0], col_count * row_count)

def convolve(padded, weights, col_count, row_count, adjoint):
    running = jnp.zeros((weights.shape[1], col_count * row_count), jnp.float32)
    for kernel_row in range(3):
        for kernel_column in range(3):
            window = tap_window(padded, kernel_row, kernel_column, adjoint, col_count, row_count)
            matrix = weights[3 * kernel_row + kernel_column]
            if adjoint:
                matrix = matrix.T
            running = running + jnp.dot(matrix, window, preferred_element_type=jnp.float32)
    return running.reshape(-1, col_count, row_count)

def weight_terms(gradient, padded, col_count, row_count):
    flattened = gradient.reshape(gradient.shape[0], -1)
    collected = []
    for kernel_row in range(3):
        for kernel_column in range(3):
            window = tap_window(padded, kernel_row, kernel_column, False, col_count, row_count)
            collected.append(lax.dot_general(flattened, window, (((1,), (1,)), ((), ())), preferred_element_type=jnp.float32))
    return jnp.stack(collected, 0)

def normalize(activation):
    cell_count = activation.shape[1] * activation.shape[2]
    average = lax.optimization_barrier(jnp.sum(activation, axis=(1, 2))) / cell_count
    centered = activation - average[:, None, None]
    spread = lax.optimization_barrier(jnp.sum(centered * centered, axis=(1, 2))) / cell_count
    inverse_std = lax.rsqrt(spread + epsilon)
    return (centered * inverse_std[:, None, None], inverse_std)

def norm_back(gradient, normed, inverse_std):
    cell_count = gradient.shape[1] * gradient.shape[2]
    first_mean = lax.optimization_barrier(jnp.sum(gradient, axis=(1, 2))) / cell_count
    second_mean = lax.optimization_barrier(jnp.sum(gradient * normed, axis=(1, 2))) / cell_count
    return inverse_std[:, None, None] * (gradient - first_mean[:, None, None] - normed * second_mean[:, None, None])

def reference(features, conv_first, conv_second, head_weight, head_bias, cotangent):
    channels, col_count, row_count = features.shape
    length = col_count
    wide_in = widen(features)
    act_first = convolve(wide_in, conv_first, col_count, row_count, False)
    normed_first, inverse_first = normalize(act_first)
    hidden_first = elu_apply(normed_first).astype(jnp.bfloat16)
    wide_hidden = widen(hidden_first)
    act_second = convolve(wide_hidden, conv_second, col_count, row_count, False)
    normed_second, inverse_second = normalize(act_second)
    summed = normed_second + features.astype(jnp.float32)
    hidden = elu_apply(summed).astype(jnp.bfloat16)
    flat_hidden = hidden.reshape(channels, -1)
    raw_logits = (jnp.dot(head_weight, flat_hidden, preferred_element_type=jnp.float32) + head_bias[:, None]).reshape(-1, col_count, row_count)
    logits = (0.5 * (raw_logits + jnp.swapaxes(raw_logits, 1, 2))).astype(jnp.bfloat16)
    cot_wide = cotangent.astype(jnp.float32)
    grad_sym = (0.5 * (cot_wide + jnp.swapaxes(cot_wide, 1, 2))).astype(jnp.bfloat16)
    flat_sym = grad_sym.reshape(grad_sym.shape[0], -1)
    bias_term = lax.optimization_barrier(jnp.sum(flat_sym, axis=1, dtype=jnp.float32))
    head_term = lax.dot_general(flat_sym, flat_hidden, (((1,), (1,)), ((), ())), preferred_element_type=jnp.float32)
    grad_hidden = jnp.dot(head_weight.T, flat_sym, preferred_element_type=jnp.float32).reshape(channels, col_count, row_count)
    grad_summed = grad_hidden * elu_slope(summed)
    grad_act_second = norm_back(grad_summed, normed_second, inverse_second).astype(jnp.bfloat16)
    second_term = weight_terms(grad_act_second, wide_hidden, col_count, row_count)
    grad_hidden_first = convolve(widen(grad_act_second), conv_second, col_count, row_count, True)
    grad_normed_first = grad_hidden_first * elu_slope(normed_first)
    grad_act_first = norm_back(grad_normed_first, normed_first, inverse_first).astype(jnp.bfloat16)
    first_term = weight_terms(grad_act_first, wide_in, col_count, row_count)
    input_grad = (convolve(widen(grad_act_first), conv_first, col_count, row_count, True) + grad_summed).astype(jnp.bfloat16)
    inverse_len = 1.0 / length
    return (logits, input_grad, first_term * inverse_len, second_term * inverse_len, head_term * inverse_len, bias_term * inverse_len)
```

```python
import functools

import jax
import jax.numpy as jnp
from jax import lax
from jax.experimental import pallas as pl
from jax.experimental.pallas import tpu as pltpu
from jax.sharding import PartitionSpec as P

DILATION_STEP = 16


epsilon = 1e-05


def with_halo(block, sides, width):
    for axis, dim in sides:
        count = lax.axis_size(axis)
        forward = [(i, i + 1) for i in range(count - 1)]
        backward = [(target, source) for source, target in forward]
        low = lax.ppermute(
            lax.slice_in_dim(block, block.shape[dim] - width, None, axis=dim), axis, forward
        )
        high = lax.ppermute(lax.slice_in_dim(block, 0, width, axis=dim), axis, backward)
        block = jnp.concatenate([low, block, high], axis=dim)
    return block


def elu_apply(value_entries):
    return jnp.where(
        value_entries > 0, value_entries, jnp.exp(jnp.minimum(value_entries, 0.0)) - 1.0
    )


def elu_slope(value_entries):
    return jnp.where(value_entries > 0, 1.0, jnp.exp(jnp.minimum(value_entries, 0.0)))


def widen(value_entries):
    return with_halo(value_entries, (("row", 2), ("col", 1)), DILATION_STEP)


def widen_grad(value_entries):
    return with_halo(value_entries, (("row", 2), ("col", 1)), DILATION_STEP)


def tap_window(padded, kernel_row, kernel_column, adjoint, col_count, row_count):
    shift_direction = -1 if adjoint else 1
    column_shift = DILATION_STEP + shift_direction * DILATION_STEP * (kernel_column - 1)
    row_shift = DILATION_STEP + shift_direction * DILATION_STEP * (kernel_row - 1)
    window = padded[:, column_shift : column_shift + col_count, row_shift : row_shift + row_count]
    return window.reshape(padded.shape[0], col_count * row_count)


def convolve(padded, weights, col_count, row_count, adjoint):
    running = jnp.zeros((weights.shape[1], col_count * row_count), jnp.float32)
    for kernel_row in range(3):
        for kernel_column in range(3):
            window = tap_window(padded, kernel_row, kernel_column, adjoint, col_count, row_count)
            matrix = weights[3 * kernel_row + kernel_column]
            if adjoint:
                matrix = matrix.T
            running = running + jnp.dot(matrix, window, preferred_element_type=jnp.float32)
    return running.reshape(-1, col_count, row_count)


def weight_terms(gradient, padded, col_count, row_count):
    flattened = gradient.reshape(gradient.shape[0], -1)
    collected = []
    for kernel_row in range(3):
        for kernel_column in range(3):
            window = tap_window(padded, kernel_row, kernel_column, False, col_count, row_count)
            collected.append(
                lax.dot_general(
                    flattened, window, (((1,), (1,)), ((), ())), preferred_element_type=jnp.float32
                )
            )
    return jnp.stack(collected, 0)


def greet(axis, count):
    me = lax.axis_index(axis)
    barrier = pltpu.get_barrier_semaphore()
    for step in range(1, count):
        pl.semaphore_signal(
            barrier,
            inc=1,
            device_id={axis: lax.rem(me + step, count)},
            device_id_type=pl.DeviceIdType.MESH,
        )


def share(axis, count, source, landing, send_sem, recv_sem):
    me = lax.axis_index(axis)
    copies = []
    for step in range(1, count):
        target = lax.rem(me + step, count)
        copy = pltpu.make_async_remote_copy(
            src_ref=source(target),
            dst_ref=landing.at[me],
            send_sem=send_sem.at[step - 1],
            recv_sem=recv_sem.at[step - 1],
            device_id={axis: target},
            device_id_type=pl.DeviceIdType.MESH,
        )
        copy.start()
        copies.append(copy)
    return copies


def finish(copies):
    for copy in copies:
        copy.wait()


def in_order(ref, count):
    total = ref[0]
    for index in range(1, count):
        total = total + ref[index]
    return total


def small_kernel(rows, cols, x_ref, o_ref, over_row, over_col, row_out, row_in, col_out, col_in):
    row, col = lax.axis_index("row"), lax.axis_index("col")
    greet("row", rows)
    greet("col", cols)
    pl.semaphore_wait(pltpu.get_barrier_semaphore(), rows + cols - 2)
    over_row[row] = x_ref[...]
    finish(share("row", rows, lambda t: over_row.at[row], over_row, row_out, row_in))
    over_col[col] = in_order(over_row, rows)
    finish(share("col", cols, lambda t: over_col.at[col], over_col, col_out, col_in))
    o_ref[...] = in_order(over_col, cols)


def large_kernel(
    rows, cols, x_ref, o_ref, parts, over_row, whole,
    part_out, part_in, row_out, row_in, col_out, col_in,
):
    row, col = lax.axis_index("row"), lax.axis_index("col")
    greet("row", rows)
    greet("col", cols)
    pl.semaphore_wait(pltpu.get_barrier_semaphore(), rows + cols - 2)
    parts[col] = x_ref[col]
    finish(share("col", cols, lambda t: x_ref.at[t], parts, part_out, part_in))
    over_row[row] = in_order(parts, cols)
    finish(share("row", rows, lambda t: over_row.at[row], over_row, row_out, row_in))
    whole[col] = in_order(over_row, rows)
    finish(share("col", cols, lambda t: whole.at[col], whole, col_out, col_in))
    o_ref[...] = whole[...]


def dma(count):
    return pltpu.SemaphoreType.DMA((count - 1,))


def sum_small(first, second, identity):
    rows, cols = lax.axis_size("row"), lax.axis_size("col")
    count = first.shape[0]
    width = -(-count // 128) * 128
    packed = jnp.pad(jnp.stack([first, second]), ((0, 6), (0, width - count)))
    total = pl.pallas_call(
        functools.partial(small_kernel, rows, cols),
        out_shape=jax.ShapeDtypeStruct((8, width), jnp.float32),
        in_specs=[pl.BlockSpec(memory_space=pltpu.VMEM)],
        out_specs=pl.BlockSpec(memory_space=pltpu.VMEM),
        scratch_shapes=[
            pltpu.VMEM((rows, 8, width), jnp.float32),
            pltpu.VMEM((cols, 8, width), jnp.float32),
            dma(rows),
            dma(rows),
            dma(cols),
            dma(cols),
        ],
        compiler_params=pltpu.CompilerParams(collective_id=identity, has_side_effects=True),
    )(packed)
    return total[0, :count], total[1, :count]


def sum_large(members, identity):
    rows, cols = lax.axis_size("row"), lax.axis_size("col")
    flat = jnp.concatenate([member.reshape(-1) for member in members])
    depth = -(-flat.shape[0] // (cols * 8 * 128)) * 8
    packed = jnp.pad(flat, (0, cols * depth * 128 - flat.shape[0])).reshape(cols, depth, 128)
    total = pl.pallas_call(
        functools.partial(large_kernel, rows, cols),
        out_shape=jax.ShapeDtypeStruct(packed.shape, jnp.float32),
        in_specs=[pl.BlockSpec(memory_space=pltpu.VMEM)],
        out_specs=pl.BlockSpec(memory_space=pltpu.VMEM),
        scratch_shapes=[
            pltpu.VMEM((cols, depth, 128), jnp.float32),
            pltpu.VMEM((rows, depth, 128), jnp.float32),
            pltpu.VMEM((cols, depth, 128), jnp.float32),
            dma(cols),
            dma(cols),
            dma(rows),
            dma(rows),
            dma(cols),
            dma(cols),
        ],
        compiler_params=pltpu.CompilerParams(collective_id=identity, has_side_effects=True),
    )(packed)
    total = total.reshape(-1)
    answers, offset = [], 0
    for member in members:
        answers.append(total[offset : offset + member.size].reshape(member.shape))
        offset += member.size
    return answers


def normalize(activation, cell_count, identity):
    totals, squares = sum_small(
        jnp.sum(activation, axis=(1, 2)), jnp.sum(activation * activation, axis=(1, 2)), identity
    )
    average = totals / cell_count
    spread = squares / cell_count - average * average
    centered = activation - average[:, None, None]
    inverse_std = lax.rsqrt(spread + epsilon)
    return (centered * inverse_std[:, None, None], inverse_std)


def norm_back(gradient, normed, inverse_std, cell_count, identity):
    first_sum, second_sum = sum_small(
        jnp.sum(gradient, axis=(1, 2)), jnp.sum(gradient * normed, axis=(1, 2)), identity
    )
    first_mean = first_sum / cell_count
    second_mean = second_sum / cell_count
    return inverse_std[:, None, None] * (
        gradient - first_mean[:, None, None] - normed * second_mean[:, None, None]
    )


def mirror(tensor):
    rows, cols = lax.axis_size("row"), lax.axis_size("col")
    ratio = cols // rows
    edge = tensor.shape[1]
    col = lax.axis_index("col")
    halves = tensor.reshape(tensor.shape[0], edge, ratio, edge).transpose(2, 0, 3, 1)
    arrived = []
    for step in range(ratio):
        pairs = [
            (r * cols + c, (c // ratio) * cols + ratio * r + (c + step) % ratio)
            for r in range(rows)
            for c in range(cols)
        ]
        mine = lax.dynamic_index_in_dim(halves, lax.rem(col + step, ratio), 0, False)
        arrived.append(lax.ppermute(mine, ("row", "col"), pairs))
    stacked = jnp.stack(arrived)
    places = lax.rem(col - jnp.arange(ratio) + ratio * cols, ratio)
    ordered = [
        lax.dynamic_index_in_dim(stacked, places[index], 0, False) for index in range(ratio)
    ]
    return jnp.concatenate(ordered, axis=2)


def on_device(features, conv_first, conv_second, head_weight, head_bias, cotangent):
    channels, col_count, row_count = features.shape
    length = col_count * lax.axis_size("col")
    cell_count = float(length * length)
    cot_mirror = mirror(cotangent)
    wide_in = widen(features)
    act_first = convolve(wide_in, conv_first, col_count, row_count, False)
    normed_first, inverse_first = normalize(act_first, cell_count, 0)
    hidden_first = elu_apply(normed_first).astype(jnp.bfloat16)
    wide_hidden = widen(hidden_first)
    act_second = convolve(wide_hidden, conv_second, col_count, row_count, False)
    normed_second, inverse_second = normalize(act_second, cell_count, 1)
    summed = normed_second + features.astype(jnp.float32)
    hidden = elu_apply(summed).astype(jnp.bfloat16)
    flat_hidden = hidden.reshape(channels, -1)
    raw_logits = (
        jnp.dot(head_weight, flat_hidden, preferred_element_type=jnp.float32) + head_bias[:, None]
    ).reshape(-1, col_count, row_count)
    logit_mirror = mirror(raw_logits.astype(jnp.bfloat16)).astype(jnp.float32)
    logits = (0.5 * (raw_logits + logit_mirror)).astype(jnp.bfloat16)
    grad_sym = (0.5 * (cotangent.astype(jnp.float32) + cot_mirror.astype(jnp.float32))).astype(
        jnp.bfloat16
    )
    flat_sym = grad_sym.reshape(grad_sym.shape[0], -1)
    bias_term = jnp.sum(flat_sym, axis=1, dtype=jnp.float32)
    head_term = lax.dot_general(
        flat_sym, flat_hidden, (((1,), (1,)), ((), ())), preferred_element_type=jnp.float32
    )
    grad_hidden = jnp.dot(head_weight.T, flat_sym, preferred_element_type=jnp.float32).reshape(
        channels, col_count, row_count
    )
    grad_summed = grad_hidden * elu_slope(summed)
    grad_act_second = norm_back(grad_summed, normed_second, inverse_second, cell_count, 2).astype(
        jnp.bfloat16
    )
    second_term = weight_terms(grad_act_second, wide_hidden, col_count, row_count)
    grad_hidden_first = convolve(
        widen_grad(grad_act_second), conv_second, col_count, row_count, True
    )
    grad_normed_first = grad_hidden_first * elu_slope(normed_first)
    grad_act_first = norm_back(
        grad_normed_first, normed_first, inverse_first, cell_count, 3
    ).astype(
        jnp.bfloat16
    )
    first_term = weight_terms(grad_act_first, wide_in, col_count, row_count)
    input_grad = (
        convolve(widen_grad(grad_act_first), conv_first, col_count, row_count, True) + grad_summed
    ).astype(jnp.bfloat16)
    reduced = sum_large((first_term, second_term, head_term, bias_term), 4)
    inverse_len = 1.0 / length
    return (
        logits,
        input_grad,
        reduced[0] * inverse_len,
        reduced[1] * inverse_len,
        reduced[2] * inverse_len,
        reduced[3] * inverse_len,
    )


def solution(mesh):
    placed = (P(None, "col", "row"), P(), P(), P(), P(), P(None, "col", "row"))
    return jax.shard_map(
        on_device,
        mesh=mesh,
        in_specs=placed,
        out_specs=(P(None, "col", "row"), P(None, "col", "row"), P(), P(), P(), P()),
        check_vma=False,
    )
```

```python
import functools

import jax
import jax.numpy as jnp
from jax import lax
from jax.experimental import pallas as pl
from jax.experimental.pallas import tpu as pltpu
from jax.sharding import PartitionSpec as P

DILATION_STEP = 16


epsilon = 1e-05


def elu_apply(value_entries):
    return jnp.where(
        value_entries > 0, value_entries, jnp.exp(jnp.minimum(value_entries, 0.0)) - 1.0
    )


def elu_slope(value_entries):
    return jnp.where(value_entries > 0, 1.0, jnp.exp(jnp.minimum(value_entries, 0.0)))


def greet(axis, count):
    me = lax.axis_index(axis)
    barrier = pltpu.get_barrier_semaphore()
    for step in range(1, count):
        pl.semaphore_signal(
            barrier,
            inc=1,
            device_id={axis: lax.rem(me + step, count)},
            device_id_type=pl.DeviceIdType.MESH,
        )


def share(axis, count, source, landing, send_sem, recv_sem):
    me = lax.axis_index(axis)
    copies = []
    for step in range(1, count):
        target = lax.rem(me + step, count)
        copy = pltpu.make_async_remote_copy(
            src_ref=source(target),
            dst_ref=landing.at[me],
            send_sem=send_sem.at[step - 1],
            recv_sem=recv_sem.at[step - 1],
            device_id={axis: target},
            device_id_type=pl.DeviceIdType.MESH,
        )
        copy.start()
        copies.append(copy)
    return copies


def finish(copies):
    for copy in copies:
        copy.wait()


def in_order(ref, count):
    total = ref[0]
    for index in range(1, count):
        total = total + ref[index]
    return total


def mirror(tensor):
    rows, cols = lax.axis_size("row"), lax.axis_size("col")
    ratio = cols // rows
    edge = tensor.shape[1]
    col = lax.axis_index("col")
    halves = tensor.reshape(tensor.shape[0], edge, ratio, edge).transpose(2, 0, 3, 1)
    arrived = []
    for step in range(ratio):
        pairs = [
            (r * cols + c, (c // ratio) * cols + ratio * r + (c + step) % ratio)
            for r in range(rows)
            for c in range(cols)
        ]
        mine = lax.dynamic_index_in_dim(halves, lax.rem(col + step, ratio), 0, False)
        arrived.append(lax.ppermute(mine, ("row", "col"), pairs))
    stacked = jnp.stack(arrived)
    places = lax.rem(col - jnp.arange(ratio) + ratio * cols, ratio)
    ordered = [
        lax.dynamic_index_in_dim(stacked, places[index], 0, False) for index in range(ratio)
    ]
    return jnp.concatenate(ordered, axis=2)


def dma(count):
    return pltpu.SemaphoreType.DMA((count,))


DIRECTIONS = ((0, -1), (0, 1), (-1, 0), (1, 0), (-1, -1), (-1, 1), (1, -1), (1, 1))


def meet(rows, cols):
    row, col = lax.axis_index("row"), lax.axis_index("col")
    greet("row", rows)
    greet("col", cols)
    barrier = pltpu.get_barrier_semaphore()
    corners = [pair for pair in DIRECTIONS if pair[0] and pair[1]]
    for down, across in corners:
        pl.semaphore_signal(
            barrier,
            inc=1,
            device_id={
                "row": lax.rem(row + rows + down, rows),
                "col": lax.rem(col + cols + across, cols),
            },
            device_id_type=pl.DeviceIdType.MESH,
        )
    pl.semaphore_wait(barrier, rows + cols - 2 + len(corners))


class Plan:
    def __init__(self, channels, height, lanes, rows, cols):
        self.channels, self.height, self.lanes = channels, height, lanes
        self.rows, self.cols = rows, cols
        self.margin = DILATION_STEP * lanes
        self.cells = height * lanes
        self.group = lanes // DILATION_STEP
        self.chunk = self.group * lanes
        self.chunks = self.cells // self.chunk
        self.width = self.cells + 2 * self.margin
        self.edge = DILATION_STEP // self.group * lanes
        self.strip = self.chunks * lanes
        self.strip_width = self.strip + 2 * self.edge

    def wide_scratch(self):
        return [
            pltpu.VMEM((self.channels, self.strip), jnp.bfloat16),
            pltpu.VMEM((self.channels, self.strip), jnp.bfloat16),
            pltpu.VMEM((self.channels, self.strip_width), jnp.bfloat16),
            pltpu.VMEM((self.channels, self.strip_width), jnp.bfloat16),
            dma(8),
            dma(8),
        ]

    def sum_scratch(self):
        return [
            pltpu.VMEM((self.rows, 8, 128), jnp.float32),
            pltpu.VMEM((self.cols, 8, 128), jnp.float32),
            dma(self.rows - 1),
            dma(self.rows - 1),
            dma(self.cols - 1),
            dma(self.cols - 1),
        ]

    def at(self, index, offset=0, size=None):
        size = self.chunk if size is None else size
        return pl.ds(pl.multiple_of(index * size + offset, 128), size)


def clear(plan, wide, low, high):
    middle = slice(plan.channels, 2 * plan.channels)
    blank = jnp.zeros((plan.channels, plan.margin), jnp.bfloat16)
    wide[middle, : plan.margin] = blank
    wide[middle, plan.width - plan.margin :] = blank
    low[...] = jnp.zeros_like(low)
    high[...] = jnp.zeros_like(high)


def emit(plan, wide, last, first, index, values):
    n, lanes, step = plan.channels, plan.lanes, DILATION_STEP
    place = plan.at(index, plan.margin)
    lane = lax.broadcasted_iota(jnp.int32, (n, lanes), 1)
    wide[n : 2 * n, place] = values.astype(jnp.bfloat16)
    later, sooner = [], []
    tail, lead = jnp.zeros((n, lanes), jnp.float32), jnp.zeros((n, lanes), jnp.float32)
    for m in range(plan.group):
        line = values[:, m * lanes : (m + 1) * lanes]
        right = pltpu.roll(line, step, 1)
        left = pltpu.roll(line, lanes - step, 1)
        later.append(right.astype(jnp.bfloat16))
        sooner.append(left.astype(jnp.bfloat16))
        mine = (lane >= m * step) & (lane < (m + 1) * step)
        tail = jnp.where(mine, pltpu.roll(right, m * step, 1) if m else right, tail)
        lead = jnp.where(mine, pltpu.roll(line, m * step, 1) if m else line, lead)
    wide[0:n, place] = jnp.concatenate(later, axis=1)
    wide[2 * n : 3 * n, place] = jnp.concatenate(sooner, axis=1)
    spot = plan.at(index, 0, lanes)
    last[:, spot] = tail.astype(jnp.bfloat16)
    first[:, spot] = lead.astype(jnp.bfloat16)


def halo_copies(plan, wide, last, first, low, high, send_sem, recv_sem):
    row, col = lax.axis_index("row"), lax.axis_index("col")
    n = plan.channels
    middle = slice(n, 2 * n)
    found = []
    for index, (down, across) in enumerate(DIRECTIONS):
        if down == 0:
            if across < 0:
                source = wide.at[middle, plan.margin : 2 * plan.margin]
                target = wide.at[middle, plan.width - plan.margin : plan.width]
            else:
                source = wide.at[middle, plan.cells : plan.cells + plan.margin]
                target = wide.at[middle, 0 : plan.margin]
        else:
            strip, landing = (last, low) if down > 0 else (first, high)
            if across == 0:
                source, target = strip, landing.at[:, plan.edge : plan.edge + plan.strip]
            elif across > 0:
                source = strip.at[:, plan.strip - plan.edge : plan.strip]
                target = landing.at[:, 0 : plan.edge]
            else:
                source = strip.at[:, 0 : plan.edge]
                target = landing.at[:, plan.edge + plan.strip : plan.strip_width]
        there = {
            "row": jnp.clip(row + down, 0, plan.rows - 1),
            "col": jnp.clip(col + across, 0, plan.cols - 1),
        }
        copy = pltpu.make_async_remote_copy(
            src_ref=source,
            dst_ref=target,
            send_sem=send_sem.at[index],
            recv_sem=recv_sem.at[index],
            device_id=there,
            device_id_type=pl.DeviceIdType.MESH,
        )

        def inside(r, c):
            return (r >= 0) & (r < plan.rows) & (c >= 0) & (c < plan.cols)

        found.append((copy, inside(row + down, col + across), inside(row - down, col - across)))
    return found


def halo_start(copies):
    for copy, sends, _ in copies:
        pl.when(sends)(copy.start)


def halo_wait(copies):
    for copy, sends, receives in copies:
        pl.when(receives)(copy.wait_recv)
        pl.when(sends)(copy.wait_send)


def mend(plan, wide, low, high):
    n, lanes, step = plan.channels, plan.lanes, DILATION_STEP
    lane = lax.broadcasted_iota(jnp.int32, (n, lanes), 1)

    def fill(index, fresh):
        place = plan.at(index)
        spot = plan.at(index, 0, lanes)
        before = low[:, spot].astype(jnp.float32)
        after = high[:, spot].astype(jnp.float32)
        middle = wide[n : 2 * n, place].astype(jnp.float32) if fresh else None
        old_later = None if fresh else wide[0:n, place].astype(jnp.float32)
        old_sooner = None if fresh else wide[2 * n : 3 * n, place].astype(jnp.float32)
        later, sooner = [], []
        for m in range(plan.group):
            line = slice(m * lanes, (m + 1) * lanes)
            if fresh:
                right = pltpu.roll(middle[:, line], step, 1)
                left = pltpu.roll(middle[:, line], lanes - step, 1)
            else:
                right, left = old_later[:, line], old_sooner[:, line]
            enter = pltpu.roll(before, (lanes - m * step) % lanes, 1) if m else before
            back = (lanes - step - m * step) % lanes
            leave = pltpu.roll(after, back, 1) if back else after
            later.append(jnp.where(lane < step, enter, right).astype(jnp.bfloat16))
            sooner.append(jnp.where(lane >= lanes - step, leave, left).astype(jnp.bfloat16))
        wide[0:n, place] = jnp.concatenate(later, axis=1)
        wide[2 * n : 3 * n, place] = jnp.concatenate(sooner, axis=1)

    side = plan.margin // plan.chunk

    def outer(index, carry):
        fill(index, True)
        fill(index + side + plan.chunks, True)
        return carry

    def inner(index, carry):
        fill(index + side, False)
        return carry

    lax.fori_loop(0, side, outer, 0)
    lax.fori_loop(0, plan.chunks, inner, 0)


def conv_chunk(plan, wide, weight, index):
    total = None
    for b in range(3):
        part = jnp.dot(
            weight[b],
            wide[:, plan.at(index, b * plan.margin)],
            preferred_element_type=jnp.float32,
        )
        total = part if total is None else total + part
    return total


def weight_chunk(plan, wide, gradient, index):
    return [
        lax.dot_general(
            gradient,
            wide[:, plan.at(index, b * plan.margin)],
            (((1,), (1,)), ((), ())),
            preferred_element_type=jnp.float32,
        )
        for b in range(3)
    ]


def total_sums(plan, pair, over_row, over_col, row_out, row_in, col_out, col_in):
    row, col = lax.axis_index("row"), lax.axis_index("col")
    n = plan.channels
    lane = lax.broadcasted_iota(jnp.int32, (n, 128), 1)
    both = jnp.where(lane == 0, pair[0], jnp.where(lane == 1, pair[1], 0.0))
    square = jnp.concatenate([both, jnp.zeros((128 - n, 128), jnp.float32)], axis=0)
    over_row[row] = square.T[0:8]
    finish(share("row", plan.rows, lambda t: over_row.at[row], over_row, row_out, row_in))
    over_col[col] = in_order(over_row, plan.rows)
    finish(share("col", plan.cols, lambda t: over_col.at[col], over_col, col_out, col_in))
    summed = in_order(over_col, plan.cols)
    back = jnp.concatenate([summed, jnp.zeros((120, 128), jnp.float32)], axis=0).T
    return back[0:n, 0:1], back[0:n, 1:2]


def pair_of(first, second):
    return jnp.sum(first, axis=1, keepdims=True), jnp.sum(second, axis=1, keepdims=True)


def forward_kernel(plan, cell_count, *refs):
    x, w_first, w_second, w_head, bias = refs[:5]
    wide_x, wide_h, n_first, n_second, raw, hidden, inv_first, inv_second = refs[5:13]
    act = refs[13]
    ends_x, ends_h = refs[14:20], refs[20:26]
    sums_first, sums_second = refs[26:32], refs[32:38]
    n = plan.channels
    zero = jnp.zeros((n, 1), jnp.float32)
    clear(plan, wide_x, ends_x[2], ends_x[3])
    clear(plan, wide_h, ends_h[2], ends_h[3])
    meet(plan.rows, plan.cols)

    def load(index, carry):
        emit(plan, wide_x, ends_x[0], ends_x[1], index, x[:, plan.at(index)].astype(jnp.float32))
        return carry

    lax.fori_loop(0, plan.chunks, load, 0)
    copies = halo_copies(plan, wide_x, *ends_x)
    halo_start(copies)
    halo_wait(copies)
    mend(plan, wide_x, ends_x[2], ends_x[3])

    def convolve(wide, weight):
        def body(index, carry):
            part = conv_chunk(plan, wide, weight, index)
            act[:, plan.at(index)] = part
            found = pair_of(part, part * part)
            return carry[0] + found[0], carry[1] + found[1]

        return lax.fori_loop(0, plan.chunks, body, (zero, zero))

    def moments(pair, scratch, kept):
        totals, squares = total_sums(plan, pair, *scratch)
        average = totals / cell_count
        inverse = lax.rsqrt(squares / cell_count - average * average + epsilon)
        kept[...] = jnp.broadcast_to(inverse, kept.shape)
        return average, inverse

    average, inverse = moments(convolve(wide_x, w_first), sums_first, inv_first)

    def middle(index, carry):
        normed = (act[:, plan.at(index)] - average) * inverse
        n_first[:, plan.at(index)] = normed
        emit(plan, wide_h, ends_h[0], ends_h[1], index, elu_apply(normed))
        return carry

    lax.fori_loop(0, plan.chunks, middle, 0)
    copies = halo_copies(plan, wide_h, *ends_h)
    halo_start(copies)
    halo_wait(copies)
    mend(plan, wide_h, ends_h[2], ends_h[3])
    average_2, inverse_2 = moments(convolve(wide_h, w_second), sums_second, inv_second)

    def tail(index, carry):
        place = plan.at(index)
        normed = (act[:, place] - average_2) * inverse_2
        n_second[:, place] = normed
        out = elu_apply(normed + x[:, place].astype(jnp.float32)).astype(jnp.bfloat16)
        hidden[:, place] = out
        raw[:, place] = (
            jnp.dot(w_head[...], out, preferred_element_type=jnp.float32) + bias[:, 0:1]
        )
        return carry

    lax.fori_loop(0, plan.chunks, tail, 0)


def backward_kernel(plan, cell_count, depth, *refs):
    (x, wide_x, wide_h, n_first, n_second, inv_first, inv_second) = refs[:7]
    sym, hidden, w_first, w_second, w_head = refs[7:12]
    grad_x, gathered = refs[12:14]
    wide_2, wide_1, slope_grad, inner_grad = refs[14:18]
    ends_2, ends_1 = refs[18:24], refs[24:30]
    sums_2, sums_1 = refs[30:36], refs[36:42]
    (mine, parts, over_row, whole, part_out, part_in) = refs[42:48]
    row_out, row_in, col_out, col_in = refs[48:52]
    row, col = lax.axis_index("row"), lax.axis_index("col")
    n, bins = plan.channels, sym.shape[0]
    zero = jnp.zeros((n, 1), jnp.float32)
    clear(plan, wide_2, ends_2[2], ends_2[3])
    clear(plan, wide_1, ends_1[2], ends_1[3])
    mine[...] = jnp.zeros_like(mine)
    meet(plan.rows, plan.cols)
    head_at = 6 * n

    def start(index, carry):
        place = plan.at(index)
        sym_part = sym[:, place]
        summed = n_second[:, place] + x[:, place].astype(jnp.float32)
        part = jnp.dot(w_head[...], sym_part, preferred_element_type=jnp.float32)
        part = part * elu_slope(summed)
        slope_grad[:, place] = part
        mine[head_at : head_at + bins, 0:n] += lax.dot_general(
            sym_part, hidden[:, place], (((1,), (1,)), ((), ())),
            preferred_element_type=jnp.float32,
        )
        mine[head_at : head_at + bins, 128:256] += jnp.broadcast_to(
            jnp.sum(sym_part.astype(jnp.float32), axis=1, keepdims=True), (bins, 128)
        )
        found = pair_of(part, part * n_second[:, place])
        return carry[0] + found[0], carry[1] + found[1]

    pair = lax.fori_loop(0, plan.chunks, start, (zero, zero))

    def step_back(pair, scratch, source, normed, inverse_ref, wide, ends):
        first_sum, second_sum = total_sums(plan, pair, *scratch)
        first_mean, second_mean = first_sum / cell_count, second_sum / cell_count
        inverse = inverse_ref[:, 0:1]

        def body(index, carry):
            place = plan.at(index)
            value = inverse * (source[:, place] - first_mean - normed[:, place] * second_mean)
            emit(plan, wide, ends[0], ends[1], index, value)
            return carry

        lax.fori_loop(0, plan.chunks, body, 0)
        copies = halo_copies(plan, wide, *ends)
        halo_start(copies)
        return copies

    def weigh(wide, against, base):
        def body(index, carry):
            gradient = wide[n : 2 * n, plan.at(index, plan.margin)]
            for b, part in enumerate(weight_chunk(plan, against, gradient, index)):
                mine[base + b * n : base + (b + 1) * n, 0 : 3 * n] += part
            return carry

        lax.fori_loop(0, plan.chunks, body, 0)

    copies = step_back(pair, sums_2, slope_grad, n_second, inv_second, wide_2, ends_2)
    weigh(wide_2, wide_h, 3 * n)
    halo_wait(copies)
    mend(plan, wide_2, ends_2[2], ends_2[3])

    def through(index, carry):
        place = plan.at(index)
        normed = n_first[:, place]
        part = conv_chunk(plan, wide_2, w_second, index) * elu_slope(normed)
        inner_grad[:, place] = part
        found = pair_of(part, part * normed)
        return carry[0] + found[0], carry[1] + found[1]

    pair = lax.fori_loop(0, plan.chunks, through, (zero, zero))
    copies = step_back(pair, sums_1, inner_grad, n_first, inv_first, wide_1, ends_1)
    weigh(wide_1, wide_x, 0)

    def piece(ref, t):
        return ref.at[pl.ds(pl.multiple_of(t * depth, 8), depth)]

    parts[col] = piece(mine, col)[...]
    sums = share("col", plan.cols, lambda t: piece(mine, t), parts, part_out, part_in)
    halo_wait(copies)
    mend(plan, wide_1, ends_1[2], ends_1[3])
    finish(sums)
    over_row[row] = in_order(parts, plan.cols)
    sums = share("row", plan.rows, lambda t: over_row.at[row], over_row, row_out, row_in)

    def last(index, carry):
        place = plan.at(index)
        part = conv_chunk(plan, wide_1, w_first, index) + slope_grad[:, place]
        grad_x[:, place] = part.astype(jnp.bfloat16)
        return carry

    lax.fori_loop(0, plan.chunks, last, 0)
    finish(sums)
    whole[col] = in_order(over_row, plan.rows)
    finish(share("col", plan.cols, lambda t: whole.at[col], whole, col_out, col_in))
    gathered[...] = whole[...]


def vmem(count):
    return [pl.BlockSpec(memory_space=pltpu.VMEM)] * count


def taps(weights, adjoint):
    count, outs, ins = weights.shape
    grid = weights.reshape(3, 3, outs, ins)
    if adjoint:
        return grid[::-1, ::-1].transpose(1, 3, 0, 2).reshape(3, ins, 3 * outs)
    return grid.transpose(1, 2, 0, 3).reshape(3, outs, 3 * ins)


def on_device(features, conv_first, conv_second, head_weight, head_bias, cotangent):
    channels, height, lanes = features.shape
    rows, cols = lax.axis_size("row"), lax.axis_size("col")
    length = height * cols
    cell_count = float(length * length)
    bins = head_weight.shape[0]
    padded = -(-bins // 16) * 16
    plan = Plan(channels, height, lanes, rows, cols)
    cells, width = plan.cells, plan.width
    cot_mirror = mirror(cotangent)
    grad_sym = (0.5 * (cotangent.astype(jnp.float32) + cot_mirror.astype(jnp.float32))).astype(
        jnp.bfloat16
    )
    sym = jnp.pad(grad_sym.reshape(bins, cells), ((0, padded - bins), (0, 0)))
    x = features.reshape(channels, cells)
    w_head = jnp.pad(head_weight, ((0, padded - bins), (0, 0)))
    bias = jnp.broadcast_to(jnp.pad(head_bias, (0, padded - bins))[:, None], (padded, 128))
    wide_shape = jax.ShapeDtypeStruct((3 * channels, width), jnp.bfloat16)
    full_shape = jax.ShapeDtypeStruct((channels, cells), jnp.float32)
    short_shape = jax.ShapeDtypeStruct((channels, cells), jnp.bfloat16)
    inverse_shape = jax.ShapeDtypeStruct((channels, 128), jnp.float32)
    flops = 2 * 9 * channels * channels * cells
    wide_x, wide_h, n_first, n_second, raw, hidden, inv_first, inv_second = pl.pallas_call(
        functools.partial(forward_kernel, plan, cell_count),
        out_shape=(
            wide_shape,
            wide_shape,
            full_shape,
            full_shape,
            jax.ShapeDtypeStruct((padded, cells), jnp.float32),
            short_shape,
            inverse_shape,
            inverse_shape,
        ),
        in_specs=vmem(5),
        out_specs=tuple(vmem(8)),
        scratch_shapes=[
            pltpu.VMEM((channels, cells), jnp.float32),
            *plan.wide_scratch(),
            *plan.wide_scratch(),
            *plan.sum_scratch(),
            *plan.sum_scratch(),
        ],
        compiler_params=pltpu.CompilerParams(
            collective_id=0, has_side_effects=True, vmem_limit_bytes=40 * 2**20
        ),
        cost_estimate=pl.CostEstimate(
            flops=20 * flops, bytes_accessed=200 * 2**20, transcendentals=0
        ),
    )(x, taps(conv_first, False), taps(conv_second, False), w_head, bias)
    raw_logits = raw[:bins].reshape(bins, height, lanes)
    logit_mirror = mirror(raw_logits.astype(jnp.bfloat16)).astype(jnp.float32)
    logits = (0.5 * (raw_logits + logit_mirror)).astype(jnp.bfloat16)
    total_rows = 6 * channels + padded
    depth = -(-total_rows // (cols * 8)) * 8
    grad_x, gathered = pl.pallas_call(
        functools.partial(backward_kernel, plan, cell_count, depth),
        out_shape=(short_shape, jax.ShapeDtypeStruct((cols, depth, 256), jnp.float32)),
        in_specs=vmem(12),
        out_specs=tuple(vmem(2)),
        scratch_shapes=[
            pltpu.VMEM(wide_shape.shape, jnp.bfloat16),
            pltpu.VMEM(wide_shape.shape, jnp.bfloat16),
            pltpu.VMEM((channels, cells), jnp.float32),
            pltpu.VMEM((channels, cells), jnp.float32),
            *plan.wide_scratch(),
            *plan.wide_scratch(),
            *plan.sum_scratch(),
            *plan.sum_scratch(),
            pltpu.VMEM((cols * depth, 256), jnp.float32),
            pltpu.VMEM((cols, depth, 256), jnp.float32),
            pltpu.VMEM((rows, depth, 256), jnp.float32),
            pltpu.VMEM((cols, depth, 256), jnp.float32),
            dma(cols - 1),
            dma(cols - 1),
            dma(rows - 1),
            dma(rows - 1),
            dma(cols - 1),
            dma(cols - 1),
        ],
        compiler_params=pltpu.CompilerParams(
            collective_id=1, has_side_effects=True, vmem_limit_bytes=52 * 2**20
        ),
        cost_estimate=pl.CostEstimate(
            flops=20 * flops, bytes_accessed=200 * 2**20, transcendentals=0
        ),
    )(
        x, wide_x, wide_h, n_first, n_second, inv_first, inv_second, sym, hidden,
        taps(conv_first, True), taps(conv_second, True), w_head.T,
    )
    inverse_len = 1.0 / length
    flat = gathered.reshape(cols * depth, 256) * inverse_len

    def kernel_grad(base):
        part = flat[base : base + 3 * channels, : 3 * channels]
        part = part.reshape(3, channels, 3, channels).transpose(2, 0, 1, 3)
        return part.reshape(9, channels, channels)

    start = 6 * channels
    return (
        logits,
        grad_x.reshape(channels, height, lanes),
        kernel_grad(0),
        kernel_grad(3 * channels),
        flat[start : start + bins, :channels],
        flat[start : start + bins, 128],
    )


def solution(mesh):
    placed = (P(None, "col", "row"), P(), P(), P(), P(), P(None, "col", "row"))
    return jax.shard_map(
        on_device,
        mesh=mesh,
        in_specs=placed,
        out_specs=(P(None, "col", "row"), P(None, "col", "row"), P(), P(), P(), P()),
        check_vma=False,
    )
```

```python
import functools

import jax
import jax.numpy as jnp
from jax import lax
from jax.experimental import pallas as pl
from jax.experimental.pallas import tpu as pltpu
from jax.sharding import PartitionSpec as P

DILATION_STEP = 16


epsilon = 1e-05


def elu_apply(value_entries):
    return jnp.where(
        value_entries > 0, value_entries, jnp.exp(jnp.minimum(value_entries, 0.0)) - 1.0
    )


def elu_slope(value_entries):
    return jnp.where(value_entries > 0, 1.0, jnp.exp(jnp.minimum(value_entries, 0.0)))


def greet(axis, count):
    me = lax.axis_index(axis)
    barrier = pltpu.get_barrier_semaphore()
    for step in range(1, count):
        pl.semaphore_signal(
            barrier,
            inc=1,
            device_id={axis: lax.rem(me + step, count)},
            device_id_type=pl.DeviceIdType.MESH,
        )


def share(axis, count, source, landing, send_sem, recv_sem):
    me = lax.axis_index(axis)
    copies = []
    for step in range(1, count):
        target = lax.rem(me + step, count)
        copy = pltpu.make_async_remote_copy(
            src_ref=source(target),
            dst_ref=landing.at[me],
            send_sem=send_sem.at[step - 1],
            recv_sem=recv_sem.at[step - 1],
            device_id={axis: target},
            device_id_type=pl.DeviceIdType.MESH,
        )
        copy.start()
        copies.append(copy)
    return copies


def finish(copies):
    for copy in copies:
        copy.wait()


def in_order(ref, count):
    total = ref[0]
    for index in range(1, count):
        total = total + ref[index]
    return total


def mirror_pack(tensor, rows):
    planes, edge, lanes = tensor.shape
    each = -(-planes // rows)
    halves = lanes // edge
    padded = jnp.pad(tensor, ((0, each * rows - planes), (0, 0), (0, 0)))
    turned = padded.reshape(rows, each, edge, halves, edge).transpose(0, 3, 1, 4, 2)
    return turned.reshape(rows, halves, each, edge * edge // 128, 128)


def mirror_unpack(arrived, planes, edge):
    rows, halves, each = arrived.shape[:3]
    turned = arrived.reshape(rows, halves, each, edge, edge).transpose(0, 2, 3, 1, 4)
    return turned.reshape(rows * each, edge, halves * edge)[:planes]


class Mirror:
    def __init__(self, rows, cols, source, landing, refs):
        self.rows, self.cols = rows, cols
        self.source, self.landing = source, landing
        self.first, self.second = refs[:2]
        self.sems = refs[2:]
        self.ratio = cols // rows
        self.copies = None

    def hop_one(self):
        row = lax.axis_index("row")
        self.first[row] = self.source[row]
        self.copies = share(
            "row", self.rows, lambda t: self.source.at[t], self.first, *self.sems[0:2]
        )

    def hop_two(self):
        finish(self.copies)
        col, ratio = lax.axis_index("col"), self.ratio
        self.second[col] = self.first[lax.div(col, ratio), lax.rem(col, ratio)]
        self.copies = share(
            "col",
            self.cols,
            lambda t: self.first.at[lax.div(t, ratio), lax.rem(t, ratio)],
            self.second,
            *self.sems[2:4],
        )

    def hop_three(self):
        finish(self.copies)
        row, ratio = lax.axis_index("row"), self.ratio
        self.landing[row] = self.second[pl.ds(row * ratio, ratio)]
        self.copies = share(
            "row",
            self.rows,
            lambda t: self.second.at[pl.ds(t * ratio, ratio)],
            self.landing,
            *self.sems[4:6],
        )

    def end(self):
        finish(self.copies)


class WeightSum:
    def __init__(self, rows, cols, depth, refs):
        self.rows, self.cols, self.depth = rows, cols, depth
        self.mine, self.parts, self.over_row, self.whole = refs[:4]
        self.sems = refs[4:]
        self.copies = None

    def piece(self, t):
        return self.mine.at[pl.ds(pl.multiple_of(t * self.depth, 8), self.depth)]

    def scatter(self):
        col = lax.axis_index("col")
        self.parts[col] = self.piece(col)[...]
        self.copies = share("col", self.cols, self.piece, self.parts, *self.sems[0:2])

    def across(self):
        finish(self.copies)
        row = lax.axis_index("row")
        self.over_row[row] = in_order(self.parts, self.cols)
        self.copies = share(
            "row", self.rows, lambda t: self.over_row.at[row], self.over_row, *self.sems[2:4]
        )

    def gather(self):
        finish(self.copies)
        col = lax.axis_index("col")
        self.whole[col] = in_order(self.over_row, self.rows)
        self.copies = share(
            "col", self.cols, lambda t: self.whole.at[col], self.whole, *self.sems[4:6]
        )

    def end(self):
        finish(self.copies)


def dma(count):
    return pltpu.SemaphoreType.DMA((count,))


DIRECTIONS = ((0, -1), (0, 1), (-1, 0), (1, 0), (-1, -1), (-1, 1), (1, -1), (1, 1))


def meet(rows, cols):
    row, col = lax.axis_index("row"), lax.axis_index("col")
    greet("row", rows)
    greet("col", cols)
    barrier = pltpu.get_barrier_semaphore()
    corners = [pair for pair in DIRECTIONS if pair[0] and pair[1]]
    for down, across in corners:
        pl.semaphore_signal(
            barrier,
            inc=1,
            device_id={
                "row": lax.rem(row + rows + down, rows),
                "col": lax.rem(col + cols + across, cols),
            },
            device_id_type=pl.DeviceIdType.MESH,
        )
    pl.semaphore_wait(barrier, rows + cols - 2 + len(corners))


class Plan:
    def __init__(self, channels, height, lanes, rows, cols):
        self.channels, self.height, self.lanes = channels, height, lanes
        self.rows, self.cols = rows, cols
        self.margin = DILATION_STEP * lanes
        self.cells = height * lanes
        self.group = lanes // DILATION_STEP
        self.chunk = self.group * lanes
        self.chunks = self.cells // self.chunk
        self.width = self.cells + 2 * self.margin
        self.edge = DILATION_STEP // self.group * lanes
        self.strip = self.chunks * lanes
        self.strip_width = self.strip + 2 * self.edge

    def wide_scratch(self):
        return [
            pltpu.VMEM((self.channels, self.strip), jnp.bfloat16),
            pltpu.VMEM((self.channels, self.strip), jnp.bfloat16),
            pltpu.VMEM((self.channels, self.strip_width), jnp.bfloat16),
            pltpu.VMEM((self.channels, self.strip_width), jnp.bfloat16),
            dma(8),
            dma(8),
        ]

    def sum_scratch(self):
        return [
            pltpu.VMEM((self.rows, 8, 128), jnp.float32),
            pltpu.VMEM((self.cols, 8, 128), jnp.float32),
            dma(self.rows - 1),
            dma(self.rows - 1),
            dma(self.cols - 1),
            dma(self.cols - 1),
        ]

    def mirror_scratch(self, packed):
        return [
            pltpu.VMEM(packed.shape, jnp.bfloat16),
            pltpu.VMEM((self.cols, *packed.shape[2:]), jnp.bfloat16),
            dma(self.rows - 1),
            dma(self.rows - 1),
            dma(self.cols - 1),
            dma(self.cols - 1),
            dma(self.rows - 1),
            dma(self.rows - 1),
        ]

    def depth(self, count):
        return -(-count // (self.cols * 8)) * 8

    def weight_scratch(self, depth):
        return [
            pltpu.VMEM((self.cols * depth, 256), jnp.float32),
            pltpu.VMEM((self.cols, depth, 256), jnp.float32),
            pltpu.VMEM((self.rows, depth, 256), jnp.float32),
            pltpu.VMEM((self.cols, depth, 256), jnp.float32),
            dma(self.cols - 1),
            dma(self.cols - 1),
            dma(self.rows - 1),
            dma(self.rows - 1),
            dma(self.cols - 1),
            dma(self.cols - 1),
        ]

    def at(self, index, offset=0, size=None):
        size = self.chunk if size is None else size
        return pl.ds(pl.multiple_of(index * size + offset, 128), size)


def clear(plan, wide, low, high):
    middle = slice(plan.channels, 2 * plan.channels)
    blank = jnp.zeros((plan.channels, plan.margin), jnp.bfloat16)
    wide[middle, : plan.margin] = blank
    wide[middle, plan.width - plan.margin :] = blank
    low[...] = jnp.zeros_like(low)
    high[...] = jnp.zeros_like(high)


def emit(plan, wide, last, first, index, values):
    n, lanes, step = plan.channels, plan.lanes, DILATION_STEP
    place = plan.at(index, plan.margin)
    lane = lax.broadcasted_iota(jnp.int32, (n, lanes), 1)
    wide[n : 2 * n, place] = values.astype(jnp.bfloat16)
    later, sooner = [], []
    tail, lead = jnp.zeros((n, lanes), jnp.float32), jnp.zeros((n, lanes), jnp.float32)
    for m in range(plan.group):
        line = values[:, m * lanes : (m + 1) * lanes]
        right = pltpu.roll(line, step, 1)
        left = pltpu.roll(line, lanes - step, 1)
        later.append(right.astype(jnp.bfloat16))
        sooner.append(left.astype(jnp.bfloat16))
        mine = (lane >= m * step) & (lane < (m + 1) * step)
        tail = jnp.where(mine, pltpu.roll(right, m * step, 1) if m else right, tail)
        lead = jnp.where(mine, pltpu.roll(line, m * step, 1) if m else line, lead)
    wide[0:n, place] = jnp.concatenate(later, axis=1)
    wide[2 * n : 3 * n, place] = jnp.concatenate(sooner, axis=1)
    spot = plan.at(index, 0, lanes)
    last[:, spot] = tail.astype(jnp.bfloat16)
    first[:, spot] = lead.astype(jnp.bfloat16)


def halo_copies(plan, wide, last, first, low, high, send_sem, recv_sem):
    row, col = lax.axis_index("row"), lax.axis_index("col")
    n = plan.channels
    middle = slice(n, 2 * n)
    found = []
    for index, (down, across) in enumerate(DIRECTIONS):
        if down == 0:
            if across < 0:
                source = wide.at[middle, plan.margin : 2 * plan.margin]
                target = wide.at[middle, plan.width - plan.margin : plan.width]
            else:
                source = wide.at[middle, plan.cells : plan.cells + plan.margin]
                target = wide.at[middle, 0 : plan.margin]
        else:
            strip, landing = (last, low) if down > 0 else (first, high)
            if across == 0:
                source, target = strip, landing.at[:, plan.edge : plan.edge + plan.strip]
            elif across > 0:
                source = strip.at[:, plan.strip - plan.edge : plan.strip]
                target = landing.at[:, 0 : plan.edge]
            else:
                source = strip.at[:, 0 : plan.edge]
                target = landing.at[:, plan.edge + plan.strip : plan.strip_width]
        there = {
            "row": jnp.clip(row + down, 0, plan.rows - 1),
            "col": jnp.clip(col + across, 0, plan.cols - 1),
        }
        copy = pltpu.make_async_remote_copy(
            src_ref=source,
            dst_ref=target,
            send_sem=send_sem.at[index],
            recv_sem=recv_sem.at[index],
            device_id=there,
            device_id_type=pl.DeviceIdType.MESH,
        )

        def inside(r, c):
            return (r >= 0) & (r < plan.rows) & (c >= 0) & (c < plan.cols)

        found.append((copy, inside(row + down, col + across), inside(row - down, col - across)))
    return found


def halo_start(copies):
    for copy, sends, _ in copies:
        pl.when(sends)(copy.start)


def halo_wait(copies):
    for copy, sends, receives in copies:
        pl.when(receives)(copy.wait_recv)
        pl.when(sends)(copy.wait_send)


def mend(plan, wide, low, high):
    n, lanes, step = plan.channels, plan.lanes, DILATION_STEP
    lane = lax.broadcasted_iota(jnp.int32, (n, lanes), 1)

    def fill(index, fresh):
        place = plan.at(index)
        spot = plan.at(index, 0, lanes)
        before = low[:, spot].astype(jnp.float32)
        after = high[:, spot].astype(jnp.float32)
        middle = wide[n : 2 * n, place].astype(jnp.float32) if fresh else None
        old_later = None if fresh else wide[0:n, place].astype(jnp.float32)
        old_sooner = None if fresh else wide[2 * n : 3 * n, place].astype(jnp.float32)
        later, sooner = [], []
        for m in range(plan.group):
            line = slice(m * lanes, (m + 1) * lanes)
            if fresh:
                right = pltpu.roll(middle[:, line], step, 1)
                left = pltpu.roll(middle[:, line], lanes - step, 1)
            else:
                right, left = old_later[:, line], old_sooner[:, line]
            enter = pltpu.roll(before, (lanes - m * step) % lanes, 1) if m else before
            back = (lanes - step - m * step) % lanes
            leave = pltpu.roll(after, back, 1) if back else after
            later.append(jnp.where(lane < step, enter, right).astype(jnp.bfloat16))
            sooner.append(jnp.where(lane >= lanes - step, leave, left).astype(jnp.bfloat16))
        wide[0:n, place] = jnp.concatenate(later, axis=1)
        wide[2 * n : 3 * n, place] = jnp.concatenate(sooner, axis=1)

    side = plan.margin // plan.chunk

    def outer(index, carry):
        fill(index, True)
        fill(index + side + plan.chunks, True)
        return carry

    def inner(index, carry):
        fill(index + side, False)
        return carry

    lax.fori_loop(0, side, outer, 0)
    lax.fori_loop(0, plan.chunks, inner, 0)


def conv_chunk(plan, wide, weight, index):
    total = None
    for b in range(3):
        part = jnp.dot(
            weight[b],
            wide[:, plan.at(index, b * plan.margin)],
            preferred_element_type=jnp.float32,
        )
        total = part if total is None else total + part
    return total


def weight_chunk(plan, wide, gradient, index):
    return [
        lax.dot_general(
            gradient,
            wide[:, plan.at(index, b * plan.margin)],
            (((1,), (1,)), ((), ())),
            preferred_element_type=jnp.float32,
        )
        for b in range(3)
    ]


def total_sums(plan, pair, over_row, over_col, row_out, row_in, col_out, col_in):
    row, col = lax.axis_index("row"), lax.axis_index("col")
    n = plan.channels
    lane = lax.broadcasted_iota(jnp.int32, (n, 128), 1)
    both = jnp.where(lane == 0, pair[0], jnp.where(lane == 1, pair[1], 0.0))
    square = jnp.concatenate([both, jnp.zeros((128 - n, 128), jnp.float32)], axis=0)
    over_row[row] = square.T[0:8]
    finish(share("row", plan.rows, lambda t: over_row.at[row], over_row, row_out, row_in))
    over_col[col] = in_order(over_row, plan.rows)
    finish(share("col", plan.cols, lambda t: over_col.at[col], over_col, col_out, col_in))
    summed = in_order(over_col, plan.cols)
    back = jnp.concatenate([summed, jnp.zeros((120, 128), jnp.float32)], axis=0).T
    return back[0:n, 0:1], back[0:n, 1:2]


def pair_of(first, second):
    return jnp.sum(first, axis=1, keepdims=True), jnp.sum(second, axis=1, keepdims=True)


def forward_kernel(plan, cell_count, *refs):
    x, k_first, k_second, w_head, bias, turned = refs[:6]
    wide_x, wide_h, n_first, n_second, raw, hidden, inv_first, inv_second, landing = refs[6:15]
    act, w_first, w_second = refs[15:18]
    ends_x, ends_h = refs[18:24], refs[24:30]
    sums_first, sums_second = refs[30:36], refs[36:42]
    mirror = Mirror(plan.rows, plan.cols, turned, landing, refs[42:50])
    n = plan.channels
    zero = jnp.zeros((n, 1), jnp.float32)
    clear(plan, wide_x, ends_x[2], ends_x[3])
    clear(plan, wide_h, ends_h[2], ends_h[3])
    meet(plan.rows, plan.cols)
    mirror.hop_one()
    build_taps(k_first, w_first, False)
    build_taps(k_second, w_second, False)

    def load(index, carry):
        emit(plan, wide_x, ends_x[0], ends_x[1], index, x[:, plan.at(index)].astype(jnp.float32))
        return carry

    lax.fori_loop(0, plan.chunks, load, 0)
    copies = halo_copies(plan, wide_x, *ends_x)
    halo_start(copies)
    halo_wait(copies)
    mend(plan, wide_x, ends_x[2], ends_x[3])

    def convolve(wide, weight):
        def body(index, carry):
            part = conv_chunk(plan, wide, weight, index)
            act[:, plan.at(index)] = part
            found = pair_of(part, part * part)
            return carry[0] + found[0], carry[1] + found[1]

        return lax.fori_loop(0, plan.chunks, body, (zero, zero))

    def moments(pair, scratch, kept):
        totals, squares = total_sums(plan, pair, *scratch)
        average = totals / cell_count
        inverse = lax.rsqrt(squares / cell_count - average * average + epsilon)
        kept[...] = jnp.broadcast_to(inverse, kept.shape)
        return average, inverse

    average, inverse = moments(convolve(wide_x, w_first), sums_first, inv_first)
    mirror.hop_two()

    def middle(index, carry):
        normed = (act[:, plan.at(index)] - average) * inverse
        n_first[:, plan.at(index)] = normed
        emit(plan, wide_h, ends_h[0], ends_h[1], index, elu_apply(normed))
        return carry

    lax.fori_loop(0, plan.chunks, middle, 0)
    copies = halo_copies(plan, wide_h, *ends_h)
    halo_start(copies)
    halo_wait(copies)
    mirror.hop_three()
    mend(plan, wide_h, ends_h[2], ends_h[3])
    average_2, inverse_2 = moments(convolve(wide_h, w_second), sums_second, inv_second)

    def tail(index, carry):
        place = plan.at(index)
        normed = (act[:, place] - average_2) * inverse_2
        n_second[:, place] = normed
        out = elu_apply(normed + x[:, place].astype(jnp.float32)).astype(jnp.bfloat16)
        hidden[:, place] = out
        raw[:, place] = (
            jnp.dot(w_head[...], out, preferred_element_type=jnp.float32) + bias[:, 0:1]
        )
        return carry

    lax.fori_loop(0, plan.chunks, tail, 0)
    mirror.end()


def backward_kernel(plan, cell_count, depths, *refs):
    (x, wide_x, wide_h, n_first, n_second, inv_first, inv_second) = refs[:7]
    sym, hidden, k_first, k_second, w_head, turned = refs[7:13]
    grad_x, sum_first, sum_second, landing = refs[13:17]
    wide_2, wide_1, slope_grad, inner_grad, w_first, w_second = refs[17:23]
    ends_2, ends_1 = refs[23:29], refs[29:35]
    sums_2, sums_1 = refs[35:41], refs[41:47]
    late = WeightSum(plan.rows, plan.cols, depths[0], refs[47:57])
    early = WeightSum(plan.rows, plan.cols, depths[1], refs[57:67])
    mirror = Mirror(plan.rows, plan.cols, turned, landing, refs[67:75])
    n, bins = plan.channels, sym.shape[0]
    zero = jnp.zeros((n, 1), jnp.float32)
    clear(plan, wide_2, ends_2[2], ends_2[3])
    clear(plan, wide_1, ends_1[2], ends_1[3])
    late.mine[...] = jnp.zeros_like(late.mine)
    early.mine[...] = jnp.zeros_like(early.mine)
    meet(plan.rows, plan.cols)
    mirror.hop_one()
    build_taps(k_first, w_first, True)
    build_taps(k_second, w_second, True)
    head_at = 3 * n

    def start(index, carry):
        place = plan.at(index)
        sym_part = sym[:, place]
        summed = n_second[:, place] + x[:, place].astype(jnp.float32)
        part = jnp.dot(w_head[...], sym_part, preferred_element_type=jnp.float32)
        part = part * elu_slope(summed)
        slope_grad[:, place] = part
        early.mine[head_at : head_at + bins, 0:n] += lax.dot_general(
            sym_part, hidden[:, place], (((1,), (1,)), ((), ())),
            preferred_element_type=jnp.float32,
        )
        early.mine[head_at : head_at + bins, 128:256] += jnp.broadcast_to(
            jnp.sum(sym_part.astype(jnp.float32), axis=1, keepdims=True), (bins, 128)
        )
        found = pair_of(part, part * n_second[:, place])
        return carry[0] + found[0], carry[1] + found[1]

    pair = lax.fori_loop(0, plan.chunks, start, (zero, zero))

    def step_back(pair, scratch, source, normed, inverse_ref, wide, ends, beside):
        first_sum, second_sum = total_sums(plan, pair, *scratch)
        beside()
        first_mean, second_mean = first_sum / cell_count, second_sum / cell_count
        inverse = inverse_ref[:, 0:1]

        def body(index, carry):
            place = plan.at(index)
            value = inverse * (source[:, place] - first_mean - normed[:, place] * second_mean)
            emit(plan, wide, ends[0], ends[1], index, value)
            return carry

        lax.fori_loop(0, plan.chunks, body, 0)
        copies = halo_copies(plan, wide, *ends)
        halo_start(copies)
        return copies

    def weigh(wide, against, table):
        def body(index, carry):
            gradient = wide[n : 2 * n, plan.at(index, plan.margin)]
            for b, part in enumerate(weight_chunk(plan, against, gradient, index)):
                table.mine[b * n : (b + 1) * n, 0 : 3 * n] += part
            return carry

        lax.fori_loop(0, plan.chunks, body, 0)

    copies = step_back(
        pair, sums_2, slope_grad, n_second, inv_second, wide_2, ends_2, mirror.hop_two
    )
    weigh(wide_2, wide_h, early)
    halo_wait(copies)
    mirror.hop_three()
    early.scatter()
    mend(plan, wide_2, ends_2[2], ends_2[3])

    def through(index, carry):
        place = plan.at(index)
        normed = n_first[:, place]
        part = conv_chunk(plan, wide_2, w_second, index) * elu_slope(normed)
        inner_grad[:, place] = part
        found = pair_of(part, part * normed)
        return carry[0] + found[0], carry[1] + found[1]

    pair = lax.fori_loop(0, plan.chunks, through, (zero, zero))
    early.across()
    copies = step_back(
        pair, sums_1, inner_grad, n_first, inv_first, wide_1, ends_1, early.gather
    )
    weigh(wide_1, wide_x, late)
    halo_wait(copies)
    late.scatter()
    mend(plan, wide_1, ends_1[2], ends_1[3])

    def last(index, carry):
        place = plan.at(index)
        part = conv_chunk(plan, wide_1, w_first, index) + slope_grad[:, place]
        grad_x[:, place] = part.astype(jnp.bfloat16)
        return carry

    half = plan.chunks // 2
    lax.fori_loop(0, half, last, 0)
    late.across()
    lax.fori_loop(half, plan.chunks, last, 0)
    late.gather()
    early.end()
    mirror.end()
    sum_second[...] = early.whole[...]
    late.end()
    sum_first[...] = late.whole[...]


def vmem(count):
    return [pl.BlockSpec(memory_space=pltpu.VMEM)] * count


def build_taps(kernel, table, adjoint):
    for b in range(3):
        parts = []
        for a in range(3):
            if adjoint:
                part = kernel[3 * (2 - a) + 2 - b].astype(jnp.float32).T
            else:
                part = kernel[3 * a + b].astype(jnp.float32)
            parts.append(part)
        table[b] = jnp.concatenate(parts, axis=1).astype(jnp.bfloat16)


def on_device(features, conv_first, conv_second, head_weight, head_bias, cotangent):
    channels, height, lanes = features.shape
    rows, cols = lax.axis_size("row"), lax.axis_size("col")
    length = height * cols
    cell_count = float(length * length)
    bins = head_weight.shape[0]
    padded = -(-bins // 16) * 16
    plan = Plan(channels, height, lanes, rows, cols)
    cells, width = plan.cells, plan.width
    x = features.reshape(channels, cells)
    w_head = jnp.pad(head_weight, ((0, padded - bins), (0, 0)))
    bias = jnp.broadcast_to(jnp.pad(head_bias, (0, padded - bins))[:, None], (padded, 128))
    wide_shape = jax.ShapeDtypeStruct((3 * channels, width), jnp.bfloat16)
    full_shape = jax.ShapeDtypeStruct((channels, cells), jnp.float32)
    short_shape = jax.ShapeDtypeStruct((channels, cells), jnp.bfloat16)
    inverse_shape = jax.ShapeDtypeStruct((channels, 128), jnp.float32)
    flops = 2 * 9 * channels * channels * cells
    turned = mirror_pack(cotangent, rows)
    landing_shape = jax.ShapeDtypeStruct(turned.shape, jnp.bfloat16)
    taps_scratch = pltpu.VMEM((3, channels, 3 * channels), jnp.bfloat16)
    wide_x, wide_h, n_first, n_second, raw, hidden, inv_first, inv_second, arrived = pl.pallas_call(
        functools.partial(forward_kernel, plan, cell_count),
        out_shape=(
            wide_shape,
            wide_shape,
            full_shape,
            full_shape,
            jax.ShapeDtypeStruct((padded, cells), jnp.float32),
            short_shape,
            inverse_shape,
            inverse_shape,
            landing_shape,
        ),
        in_specs=vmem(6),
        out_specs=tuple(vmem(9)),
        scratch_shapes=[
            pltpu.VMEM((channels, cells), jnp.float32),
            taps_scratch,
            taps_scratch,
            *plan.wide_scratch(),
            *plan.wide_scratch(),
            *plan.sum_scratch(),
            *plan.sum_scratch(),
            *plan.mirror_scratch(turned),
        ],
        compiler_params=pltpu.CompilerParams(
            collective_id=0, has_side_effects=True, vmem_limit_bytes=40 * 2**20
        ),
        cost_estimate=pl.CostEstimate(
            flops=20 * flops, bytes_accessed=200 * 2**20, transcendentals=0
        ),
    )(x, conv_first, conv_second, w_head, bias, turned)
    cot_mirror = mirror_unpack(arrived, bins, height)
    grad_sym = (0.5 * (cotangent.astype(jnp.float32) + cot_mirror.astype(jnp.float32))).astype(
        jnp.bfloat16
    )
    sym = jnp.pad(grad_sym.reshape(bins, cells), ((0, padded - bins), (0, 0)))
    raw_logits = raw[:bins].reshape(bins, height, lanes)
    turned = mirror_pack(raw_logits.astype(jnp.bfloat16), rows)
    depths = (plan.depth(3 * channels), plan.depth(3 * channels + padded))
    sum_shapes = [jax.ShapeDtypeStruct((cols, depth, 256), jnp.float32) for depth in depths]
    grad_x, sum_first, sum_second, arrived = pl.pallas_call(
        functools.partial(backward_kernel, plan, cell_count, depths),
        out_shape=(short_shape, *sum_shapes, landing_shape),
        in_specs=vmem(13),
        out_specs=tuple(vmem(4)),
        scratch_shapes=[
            pltpu.VMEM(wide_shape.shape, jnp.bfloat16),
            pltpu.VMEM(wide_shape.shape, jnp.bfloat16),
            pltpu.VMEM((channels, cells), jnp.float32),
            pltpu.VMEM((channels, cells), jnp.float32),
            taps_scratch,
            taps_scratch,
            *plan.wide_scratch(),
            *plan.wide_scratch(),
            *plan.sum_scratch(),
            *plan.sum_scratch(),
            *plan.weight_scratch(depths[0]),
            *plan.weight_scratch(depths[1]),
            *plan.mirror_scratch(turned),
        ],
        compiler_params=pltpu.CompilerParams(
            collective_id=1, has_side_effects=True, vmem_limit_bytes=52 * 2**20
        ),
        cost_estimate=pl.CostEstimate(
            flops=20 * flops, bytes_accessed=200 * 2**20, transcendentals=0
        ),
    )(
        x, wide_x, wide_h, n_first, n_second, inv_first, inv_second, sym, hidden,
        conv_first, conv_second, w_head.T, turned,
    )
    logit_mirror = mirror_unpack(arrived, bins, height).astype(jnp.float32)
    logits = (0.5 * (raw_logits + logit_mirror)).astype(jnp.bfloat16)
    inverse_len = 1.0 / length

    def kernel_grad(table):
        part = table[: 3 * channels, : 3 * channels] * inverse_len
        part = part.reshape(3, channels, 3, channels).transpose(2, 0, 1, 3)
        return part.reshape(9, channels, channels)

    sum_first, sum_second = sum_first.reshape(-1, 256), sum_second.reshape(-1, 256)
    head = sum_second[3 * channels : 3 * channels + bins] * inverse_len
    return (
        logits,
        grad_x.reshape(channels, height, lanes),
        kernel_grad(sum_first),
        kernel_grad(sum_second),
        head[:, :channels],
        head[:, 128],
    )


def solution(mesh):
    placed = (P(None, "col", "row"), P(), P(), P(), P(), P(None, "col", "row"))
    return jax.shard_map(
        on_device,
        mesh=mesh,
        in_specs=placed,
        out_specs=(P(None, "col", "row"), P(None, "col", "row"), P(), P(), P(), P()),
        check_vma=False,
    )
```

```python
import functools

import jax
import jax.numpy as jnp
from jax import lax
from jax.experimental import pallas as pl
from jax.experimental.pallas import tpu as pltpu
from jax.sharding import PartitionSpec as P

DILATION_STEP = 16


epsilon = 1e-05


def elu_apply(value_entries):
    return jnp.where(
        value_entries > 0, value_entries, jnp.exp(jnp.minimum(value_entries, 0.0)) - 1.0
    )


def elu_slope(value_entries):
    return jnp.where(value_entries > 0, 1.0, jnp.exp(jnp.minimum(value_entries, 0.0)))


def greet(axis, count):
    me = lax.axis_index(axis)
    barrier = pltpu.get_barrier_semaphore()
    for step in range(1, count):
        pl.semaphore_signal(
            barrier,
            inc=1,
            device_id={axis: lax.rem(me + step, count)},
            device_id_type=pl.DeviceIdType.MESH,
        )


def share(axis, count, source, landing, send_sem, recv_sem):
    me = lax.axis_index(axis)
    copies = []
    for step in range(1, count):
        target = lax.rem(me + step, count)
        copy = pltpu.make_async_remote_copy(
            src_ref=source(target),
            dst_ref=landing.at[me],
            send_sem=send_sem.at[step - 1],
            recv_sem=recv_sem.at[step - 1],
            device_id={axis: target},
            device_id_type=pl.DeviceIdType.MESH,
        )
        copy.start()
        copies.append(copy)
    return copies


def finish(copies):
    for copy in copies:
        copy.wait()


def in_order(ref, count):
    total = ref[0]
    for index in range(1, count):
        total = total + ref[index]
    return total


def mirror_pack(tensor, rows):
    planes, edge, lanes = tensor.shape
    each = -(-planes // rows)
    halves = lanes // edge
    padded = jnp.pad(tensor, ((0, each * rows - planes), (0, 0), (0, 0)))
    turned = padded.reshape(rows, each, edge, lanes).transpose(0, 1, 3, 2)
    fold, deep = 128 // edge, edge * edge // 128
    pieces = []
    for half in range(halves):
        first = half * edge
        parts = [
            turned[:, :, first + u * deep : first + (u + 1) * deep] for u in range(fold)
        ]
        pieces.append(jnp.concatenate(parts, axis=3))
    return jnp.stack(pieces, axis=1)


def mirror_unpack(arrived, planes, edge):
    rows, halves, each = arrived.shape[:3]
    fold = 128 // edge
    sides = []
    for half in range(halves):
        parts = [arrived[:, half, :, :, u * edge : (u + 1) * edge] for u in range(fold)]
        sides.append(jnp.concatenate(parts, axis=2))
    return jnp.concatenate(sides, axis=3).reshape(rows * each, edge, halves * edge)[:planes]


class Mirror:
    def __init__(self, rows, cols, source, landing, refs):
        self.rows, self.cols = rows, cols
        self.source, self.landing = source, landing
        self.first, self.second = refs[:2]
        self.sems = refs[2:]
        self.ratio = cols // rows
        self.copies = None

    def hop_one(self):
        row = lax.axis_index("row")
        self.first[row] = self.source[row]
        self.copies = share(
            "row", self.rows, lambda t: self.source.at[t], self.first, *self.sems[0:2]
        )

    def hop_two(self):
        finish(self.copies)
        col, ratio = lax.axis_index("col"), self.ratio
        self.second[col] = self.first[lax.div(col, ratio), lax.rem(col, ratio)]
        self.copies = share(
            "col",
            self.cols,
            lambda t: self.first.at[lax.div(t, ratio), lax.rem(t, ratio)],
            self.second,
            *self.sems[2:4],
        )

    def hop_three(self):
        finish(self.copies)
        row, ratio = lax.axis_index("row"), self.ratio
        self.landing[row] = self.second[pl.ds(row * ratio, ratio)]
        self.copies = share(
            "row",
            self.rows,
            lambda t: self.second.at[pl.ds(t * ratio, ratio)],
            self.landing,
            *self.sems[4:6],
        )

    def end(self):
        finish(self.copies)


class WeightSum:
    def __init__(self, rows, cols, depth, refs):
        self.rows, self.cols, self.depth = rows, cols, depth
        self.mine, self.parts, self.over_row, self.whole = refs[:4]
        self.sems = refs[4:]
        self.copies = None

    def piece(self, t):
        return self.mine.at[pl.ds(pl.multiple_of(t * self.depth, 8), self.depth)]

    def scatter(self):
        col = lax.axis_index("col")
        self.parts[col] = self.piece(col)[...]
        self.copies = share("col", self.cols, self.piece, self.parts, *self.sems[0:2])

    def across(self):
        finish(self.copies)
        row = lax.axis_index("row")
        self.over_row[row] = in_order(self.parts, self.cols)
        self.copies = share(
            "row", self.rows, lambda t: self.over_row.at[row], self.over_row, *self.sems[2:4]
        )

    def gather(self):
        finish(self.copies)
        col = lax.axis_index("col")
        self.whole[col] = in_order(self.over_row, self.rows)
        self.copies = share(
            "col", self.cols, lambda t: self.whole.at[col], self.whole, *self.sems[4:6]
        )

    def end(self):
        finish(self.copies)


def dma(count):
    return pltpu.SemaphoreType.DMA((count,))


DIRECTIONS = ((0, -1), (0, 1), (-1, 0), (1, 0), (-1, -1), (-1, 1), (1, -1), (1, 1))


def meet(rows, cols):
    row, col = lax.axis_index("row"), lax.axis_index("col")
    greet("row", rows)
    greet("col", cols)
    barrier = pltpu.get_barrier_semaphore()
    corners = [pair for pair in DIRECTIONS if pair[0] and pair[1]]
    for down, across in corners:
        pl.semaphore_signal(
            barrier,
            inc=1,
            device_id={
                "row": lax.rem(row + rows + down, rows),
                "col": lax.rem(col + cols + across, cols),
            },
            device_id_type=pl.DeviceIdType.MESH,
        )
    pl.semaphore_wait(barrier, rows + cols - 2 + len(corners))


class Plan:
    def __init__(self, channels, height, lanes, rows, cols):
        self.channels, self.height, self.lanes = channels, height, lanes
        self.rows, self.cols = rows, cols
        self.margin = DILATION_STEP * lanes
        self.cells = height * lanes
        self.group = lanes // DILATION_STEP
        self.chunk = self.group * lanes
        self.chunks = self.cells // self.chunk
        self.width = self.cells + 2 * self.margin
        self.edge = DILATION_STEP // self.group * lanes
        self.strip = self.chunks * lanes
        self.strip_width = self.strip + 2 * self.edge

    def wide_scratch(self):
        return [
            pltpu.VMEM((self.channels, self.strip), jnp.bfloat16),
            pltpu.VMEM((self.channels, self.strip), jnp.bfloat16),
            pltpu.VMEM((self.channels, self.strip_width), jnp.bfloat16),
            pltpu.VMEM((self.channels, self.strip_width), jnp.bfloat16),
            dma(8),
            dma(8),
        ]

    def sum_scratch(self):
        return [
            pltpu.VMEM((self.rows, 8, 128), jnp.float32),
            pltpu.VMEM((self.cols, 8, 128), jnp.float32),
            dma(self.rows - 1),
            dma(self.rows - 1),
            dma(self.cols - 1),
            dma(self.cols - 1),
        ]

    def mirror_scratch(self, packed):
        return [
            pltpu.VMEM(packed.shape, jnp.bfloat16),
            pltpu.VMEM((self.cols, *packed.shape[2:]), jnp.bfloat16),
            dma(self.rows - 1),
            dma(self.rows - 1),
            dma(self.cols - 1),
            dma(self.cols - 1),
            dma(self.rows - 1),
            dma(self.rows - 1),
        ]

    def depth(self, count):
        return -(-count // (self.cols * 8)) * 8

    def weight_scratch(self, depth):
        return [
            pltpu.VMEM((self.cols * depth, 128), jnp.float32),
            pltpu.VMEM((self.cols, depth, 128), jnp.float32),
            pltpu.VMEM((self.rows, depth, 128), jnp.float32),
            pltpu.VMEM((self.cols, depth, 128), jnp.float32),
            dma(self.cols - 1),
            dma(self.cols - 1),
            dma(self.rows - 1),
            dma(self.rows - 1),
            dma(self.cols - 1),
            dma(self.cols - 1),
        ]

    def at(self, index, offset=0, size=None):
        size = self.chunk if size is None else size
        return pl.ds(pl.multiple_of(index * size + offset, 128), size)


def clear(plan, wide, low, high):
    middle = slice(plan.channels, 2 * plan.channels)
    blank = jnp.zeros((plan.channels, plan.margin), jnp.bfloat16)
    wide[middle, : plan.margin] = blank
    wide[middle, plan.width - plan.margin :] = blank
    low[...] = jnp.zeros_like(low)
    high[...] = jnp.zeros_like(high)


def emit(plan, wide, last, first, index, values):
    n, lanes, step = plan.channels, plan.lanes, DILATION_STEP
    place = plan.at(index, plan.margin)
    lane = lax.broadcasted_iota(jnp.int32, (n, lanes), 1)
    wide[n : 2 * n, place] = values.astype(jnp.bfloat16)
    later, sooner = [], []
    tail, lead = jnp.zeros((n, lanes), jnp.float32), jnp.zeros((n, lanes), jnp.float32)
    for m in range(plan.group):
        line = values[:, m * lanes : (m + 1) * lanes]
        right = pltpu.roll(line, step, 1)
        left = pltpu.roll(line, lanes - step, 1)
        later.append(right.astype(jnp.bfloat16))
        sooner.append(left.astype(jnp.bfloat16))
        mine = (lane >= m * step) & (lane < (m + 1) * step)
        tail = jnp.where(mine, pltpu.roll(right, m * step, 1) if m else right, tail)
        lead = jnp.where(mine, pltpu.roll(line, m * step, 1) if m else line, lead)
    wide[0:n, place] = jnp.concatenate(later, axis=1)
    wide[2 * n : 3 * n, place] = jnp.concatenate(sooner, axis=1)
    spot = plan.at(index, 0, lanes)
    last[:, spot] = tail.astype(jnp.bfloat16)
    first[:, spot] = lead.astype(jnp.bfloat16)


def halo_copies(plan, wide, last, first, low, high, send_sem, recv_sem):
    row, col = lax.axis_index("row"), lax.axis_index("col")
    n = plan.channels
    middle = slice(n, 2 * n)
    found = []
    for index, (down, across) in enumerate(DIRECTIONS):
        if down == 0:
            if across < 0:
                source = wide.at[middle, plan.margin : 2 * plan.margin]
                target = wide.at[middle, plan.width - plan.margin : plan.width]
            else:
                source = wide.at[middle, plan.cells : plan.cells + plan.margin]
                target = wide.at[middle, 0 : plan.margin]
        else:
            strip, landing = (last, low) if down > 0 else (first, high)
            if across == 0:
                source, target = strip, landing.at[:, plan.edge : plan.edge + plan.strip]
            elif across > 0:
                source = strip.at[:, plan.strip - plan.edge : plan.strip]
                target = landing.at[:, 0 : plan.edge]
            else:
                source = strip.at[:, 0 : plan.edge]
                target = landing.at[:, plan.edge + plan.strip : plan.strip_width]
        there = {
            "row": jnp.clip(row + down, 0, plan.rows - 1),
            "col": jnp.clip(col + across, 0, plan.cols - 1),
        }
        copy = pltpu.make_async_remote_copy(
            src_ref=source,
            dst_ref=target,
            send_sem=send_sem.at[index],
            recv_sem=recv_sem.at[index],
            device_id=there,
            device_id_type=pl.DeviceIdType.MESH,
        )

        def inside(r, c):
            return (r >= 0) & (r < plan.rows) & (c >= 0) & (c < plan.cols)

        found.append((copy, inside(row + down, col + across), inside(row - down, col - across)))
    return found


def halo_start(copies):
    for copy, sends, _ in copies:
        pl.when(sends)(copy.start)


def halo_wait(copies):
    for copy, sends, receives in copies:
        pl.when(receives)(copy.wait_recv)
        pl.when(sends)(copy.wait_send)


def mend(plan, wide, low, high):
    n, lanes, step = plan.channels, plan.lanes, DILATION_STEP
    lane = lax.broadcasted_iota(jnp.int32, (n, lanes), 1)

    def fill(index, fresh):
        place = plan.at(index)
        spot = plan.at(index, 0, lanes)
        before = low[:, spot].astype(jnp.float32)
        after = high[:, spot].astype(jnp.float32)
        middle = wide[n : 2 * n, place].astype(jnp.float32) if fresh else None
        old_later = None if fresh else wide[0:n, place].astype(jnp.float32)
        old_sooner = None if fresh else wide[2 * n : 3 * n, place].astype(jnp.float32)
        later, sooner = [], []
        for m in range(plan.group):
            line = slice(m * lanes, (m + 1) * lanes)
            if fresh:
                right = pltpu.roll(middle[:, line], step, 1)
                left = pltpu.roll(middle[:, line], lanes - step, 1)
            else:
                right, left = old_later[:, line], old_sooner[:, line]
            enter = pltpu.roll(before, (lanes - m * step) % lanes, 1) if m else before
            back = (lanes - step - m * step) % lanes
            leave = pltpu.roll(after, back, 1) if back else after
            later.append(jnp.where(lane < step, enter, right).astype(jnp.bfloat16))
            sooner.append(jnp.where(lane >= lanes - step, leave, left).astype(jnp.bfloat16))
        wide[0:n, place] = jnp.concatenate(later, axis=1)
        wide[2 * n : 3 * n, place] = jnp.concatenate(sooner, axis=1)

    side = plan.margin // plan.chunk

    def outer(index, carry):
        fill(index, True)
        fill(index + side + plan.chunks, True)
        return carry

    def inner(index, carry):
        fill(index + side, False)
        return carry

    lax.fori_loop(0, side, outer, 0)
    lax.fori_loop(0, plan.chunks, inner, 0)


def conv_chunk(plan, wide, weight, index):
    total = None
    for b in range(3):
        part = jnp.dot(
            weight[b],
            wide[:, plan.at(index, b * plan.margin)],
            preferred_element_type=jnp.float32,
        )
        total = part if total is None else total + part
    return total


def weight_chunk(plan, wide, gradient, index):
    windows = [wide[:, plan.at(index, b * plan.margin)] for b in range(3)]
    return lax.dot_general(
        jnp.concatenate(windows, axis=0),
        gradient,
        (((1,), (1,)), ((), ())),
        preferred_element_type=jnp.float32,
    )


def total_sums(plan, pair, over_row, over_col, row_out, row_in, col_out, col_in):
    row, col = lax.axis_index("row"), lax.axis_index("col")
    n = plan.channels
    lane = lax.broadcasted_iota(jnp.int32, (n, 128), 1)
    both = jnp.where(lane == 0, pair[0], jnp.where(lane == 1, pair[1], 0.0))
    square = jnp.concatenate([both, jnp.zeros((128 - n, 128), jnp.float32)], axis=0)
    over_row[row] = square.T[0:8]
    finish(share("row", plan.rows, lambda t: over_row.at[row], over_row, row_out, row_in))
    over_col[col] = in_order(over_row, plan.rows)
    finish(share("col", plan.cols, lambda t: over_col.at[col], over_col, col_out, col_in))
    summed = in_order(over_col, plan.cols)
    back = jnp.concatenate([summed, jnp.zeros((120, 128), jnp.float32)], axis=0).T
    return back[0:n, 0:1], back[0:n, 1:2]


def pair_of(first, second):
    return jnp.sum(first, axis=1, keepdims=True), jnp.sum(second, axis=1, keepdims=True)


def forward_kernel(plan, cell_count, *refs):
    x, k_first, k_second, w_head, bias, turned = refs[:6]
    wide_x, wide_h, n_first, n_second, raw, hidden, inv_first, inv_second, landing = refs[6:15]
    act, w_first, w_second = refs[15:18]
    ends_x, ends_h = refs[18:24], refs[24:30]
    sums_first, sums_second = refs[30:36], refs[36:42]
    mirror = Mirror(plan.rows, plan.cols, turned, landing, refs[42:50])
    n = plan.channels
    zero = jnp.zeros((n, 1), jnp.float32)
    clear(plan, wide_x, ends_x[2], ends_x[3])
    clear(plan, wide_h, ends_h[2], ends_h[3])
    meet(plan.rows, plan.cols)
    build_taps(k_first, w_first, False)
    build_taps(k_second, w_second, False)

    def load(index, carry):
        emit(plan, wide_x, ends_x[0], ends_x[1], index, x[:, plan.at(index)].astype(jnp.float32))
        return carry

    lax.fori_loop(0, plan.chunks, load, 0)
    copies = halo_copies(plan, wide_x, *ends_x)
    halo_start(copies)
    halo_wait(copies)
    mirror.hop_one()
    mend(plan, wide_x, ends_x[2], ends_x[3])

    def convolve(wide, weight):
        def body(index, carry):
            part = conv_chunk(plan, wide, weight, index)
            act[:, plan.at(index)] = part
            found = pair_of(part, part * part)
            return carry[0] + found[0], carry[1] + found[1]

        return lax.fori_loop(0, plan.chunks, body, (zero, zero))

    def moments(pair, scratch, kept):
        totals, squares = total_sums(plan, pair, *scratch)
        average = totals / cell_count
        inverse = lax.rsqrt(squares / cell_count - average * average + epsilon)
        kept[...] = jnp.broadcast_to(inverse, kept.shape)
        return average, inverse

    average, inverse = moments(convolve(wide_x, w_first), sums_first, inv_first)
    mirror.hop_two()

    def middle(index, carry):
        normed = (act[:, plan.at(index)] - average) * inverse
        n_first[:, plan.at(index)] = normed
        emit(plan, wide_h, ends_h[0], ends_h[1], index, elu_apply(normed))
        return carry

    lax.fori_loop(0, plan.chunks, middle, 0)
    copies = halo_copies(plan, wide_h, *ends_h)
    halo_start(copies)
    halo_wait(copies)
    mend(plan, wide_h, ends_h[2], ends_h[3])
    mirror.hop_three()
    average_2, inverse_2 = moments(convolve(wide_h, w_second), sums_second, inv_second)

    def tail(index, carry):
        place = plan.at(index)
        normed = (act[:, place] - average_2) * inverse_2
        n_second[:, place] = normed
        out = elu_apply(normed + x[:, place].astype(jnp.float32)).astype(jnp.bfloat16)
        hidden[:, place] = out
        raw[:, place] = (
            jnp.dot(w_head[...], out, preferred_element_type=jnp.float32) + bias[:, 0:1]
        )
        return carry

    lax.fori_loop(0, plan.chunks, tail, 0)
    mirror.end()


def backward_kernel(plan, cell_count, depths, *refs):
    (x, wide_x, wide_h, n_first, n_second, inv_first, inv_second) = refs[:7]
    sym, hidden, k_first, k_second, w_head, turned = refs[7:13]
    grad_x, sum_first, sum_second, landing = refs[13:17]
    wide_2, wide_1, slope_grad, inner_grad, w_first, w_second = refs[17:23]
    ends_2, ends_1 = refs[23:29], refs[29:35]
    sums_2, sums_1 = refs[35:41], refs[41:47]
    late = WeightSum(plan.rows, plan.cols, depths[0], refs[47:57])
    early = WeightSum(plan.rows, plan.cols, depths[1], refs[57:67])
    mirror = Mirror(plan.rows, plan.cols, turned, landing, refs[67:75])
    piled = refs[75]
    n, bins = plan.channels, sym.shape[0]
    folded = 9 * n // 2
    zero = jnp.zeros((n, 1), jnp.float32)
    clear(plan, wide_2, ends_2[2], ends_2[3])
    clear(plan, wide_1, ends_1[2], ends_1[3])
    late.mine[...] = jnp.zeros_like(late.mine)
    early.mine[...] = jnp.zeros_like(early.mine)
    meet(plan.rows, plan.cols)
    mirror.hop_one()
    build_taps(k_first, w_first, True)
    build_taps(k_second, w_second, True)
    head_at = folded

    def start(index, carry):
        place = plan.at(index)
        sym_part = sym[:, place]
        summed = n_second[:, place] + x[:, place].astype(jnp.float32)
        part = jnp.dot(w_head[...], sym_part, preferred_element_type=jnp.float32)
        part = part * elu_slope(summed)
        slope_grad[:, place] = part
        early.mine[head_at : head_at + bins, 0:n] += lax.dot_general(
            sym_part, hidden[:, place], (((1,), (1,)), ((), ())),
            preferred_element_type=jnp.float32,
        )
        early.mine[head_at : head_at + bins, n:] += jnp.broadcast_to(
            jnp.sum(sym_part.astype(jnp.float32), axis=1, keepdims=True), (bins, 128 - n)
        )
        found = pair_of(part, part * n_second[:, place])
        return carry[0] + found[0], carry[1] + found[1]

    pair = lax.fori_loop(0, plan.chunks, start, (zero, zero))

    def step_back(pair, scratch, source, normed, inverse_ref, wide, ends, beside):
        first_sum, second_sum = total_sums(plan, pair, *scratch)
        beside()
        first_mean, second_mean = first_sum / cell_count, second_sum / cell_count
        inverse = inverse_ref[:, 0:1]

        def body(index, carry):
            place = plan.at(index)
            value = inverse * (source[:, place] - first_mean - normed[:, place] * second_mean)
            emit(plan, wide, ends[0], ends[1], index, value)
            return carry

        lax.fori_loop(0, plan.chunks, body, 0)
        copies = halo_copies(plan, wide, *ends)
        halo_start(copies)
        return copies

    def weigh(wide, against, table):
        def body(index, carry):
            gradient = wide[n : 2 * n, plan.at(index, plan.margin)]
            piled[...] += weight_chunk(plan, against, gradient, index)
            return carry

        piled[...] = jnp.zeros_like(piled)
        lax.fori_loop(0, plan.chunks, body, 0)
        table.mine[0:folded, :] = jnp.concatenate([piled[0:folded], piled[folded:]], axis=1)

    copies = step_back(
        pair, sums_2, slope_grad, n_second, inv_second, wide_2, ends_2, mirror.hop_two
    )
    weigh(wide_2, wide_h, early)
    halo_wait(copies)
    mend(plan, wide_2, ends_2[2], ends_2[3])
    mirror.hop_three()
    early.scatter()

    def through(index, carry):
        place = plan.at(index)
        normed = n_first[:, place]
        part = conv_chunk(plan, wide_2, w_second, index) * elu_slope(normed)
        inner_grad[:, place] = part
        found = pair_of(part, part * normed)
        return carry[0] + found[0], carry[1] + found[1]

    pair = lax.fori_loop(0, plan.chunks, through, (zero, zero))
    early.across()
    copies = step_back(
        pair, sums_1, inner_grad, n_first, inv_first, wide_1, ends_1, early.gather
    )
    weigh(wide_1, wide_x, late)
    halo_wait(copies)
    late.scatter()
    mend(plan, wide_1, ends_1[2], ends_1[3])

    def last(index, carry):
        place = plan.at(index)
        part = conv_chunk(plan, wide_1, w_first, index) + slope_grad[:, place]
        grad_x[:, place] = part.astype(jnp.bfloat16)
        return carry

    half = plan.chunks // 2
    lax.fori_loop(0, half, last, 0)
    late.across()
    lax.fori_loop(half, plan.chunks, last, 0)
    late.gather()
    early.end()
    mirror.end()
    sum_second[...] = early.whole[...]
    late.end()
    sum_first[...] = late.whole[...]


def vmem(count):
    return [pl.BlockSpec(memory_space=pltpu.VMEM)] * count


def build_taps(kernel, table, adjoint):
    for b in range(3):
        parts = []
        for a in range(3):
            if adjoint:
                part = kernel[3 * (2 - a) + 2 - b].astype(jnp.float32).T
            else:
                part = kernel[3 * a + b].astype(jnp.float32)
            parts.append(part)
        table[b] = jnp.concatenate(parts, axis=1).astype(jnp.bfloat16)


def on_device(features, conv_first, conv_second, head_weight, head_bias, cotangent):
    channels, height, lanes = features.shape
    rows, cols = lax.axis_size("row"), lax.axis_size("col")
    length = height * cols
    cell_count = float(length * length)
    bins = head_weight.shape[0]
    padded = -(-bins // 16) * 16
    plan = Plan(channels, height, lanes, rows, cols)
    cells, width = plan.cells, plan.width
    x = features.reshape(channels, cells)
    w_head = jnp.pad(head_weight, ((0, padded - bins), (0, 0)))
    bias = jnp.broadcast_to(jnp.pad(head_bias, (0, padded - bins))[:, None], (padded, 128))
    wide_shape = jax.ShapeDtypeStruct((3 * channels, width), jnp.bfloat16)
    full_shape = jax.ShapeDtypeStruct((channels, cells), jnp.float32)
    short_shape = jax.ShapeDtypeStruct((channels, cells), jnp.bfloat16)
    inverse_shape = jax.ShapeDtypeStruct((channels, 128), jnp.float32)
    flops = 2 * 9 * channels * channels * cells
    turned = mirror_pack(cotangent, rows)
    landing_shape = jax.ShapeDtypeStruct(turned.shape, jnp.bfloat16)
    taps_scratch = pltpu.VMEM((3, channels, 3 * channels), jnp.bfloat16)
    wide_x, wide_h, n_first, n_second, raw, hidden, inv_first, inv_second, arrived = pl.pallas_call(
        functools.partial(forward_kernel, plan, cell_count),
        out_shape=(
            wide_shape,
            wide_shape,
            full_shape,
            full_shape,
            jax.ShapeDtypeStruct((padded, cells), jnp.float32),
            short_shape,
            inverse_shape,
            inverse_shape,
            landing_shape,
        ),
        in_specs=vmem(6),
        out_specs=tuple(vmem(9)),
        scratch_shapes=[
            pltpu.VMEM((channels, cells), jnp.float32),
            taps_scratch,
            taps_scratch,
            *plan.wide_scratch(),
            *plan.wide_scratch(),
            *plan.sum_scratch(),
            *plan.sum_scratch(),
            *plan.mirror_scratch(turned),
        ],
        compiler_params=pltpu.CompilerParams(
            collective_id=0, has_side_effects=True, vmem_limit_bytes=32 * 2**20
        ),
        cost_estimate=pl.CostEstimate(
            flops=20 * flops, bytes_accessed=200 * 2**20, transcendentals=0
        ),
    )(x, conv_first, conv_second, w_head, bias, turned)
    cot_mirror = mirror_unpack(arrived, bins, height)
    grad_sym = (0.5 * (cotangent.astype(jnp.float32) + cot_mirror.astype(jnp.float32))).astype(
        jnp.bfloat16
    )
    sym = jnp.pad(grad_sym.reshape(bins, cells), ((0, padded - bins), (0, 0)))
    raw_logits = raw[:bins].reshape(bins, height, lanes)
    turned = mirror_pack(raw_logits.astype(jnp.bfloat16), rows)
    folded = 9 * channels // 2
    depths = (plan.depth(folded), plan.depth(folded + padded))
    sum_shapes = [jax.ShapeDtypeStruct((cols, depth, 128), jnp.float32) for depth in depths]
    grad_x, sum_first, sum_second, arrived = pl.pallas_call(
        functools.partial(backward_kernel, plan, cell_count, depths),
        out_shape=(short_shape, *sum_shapes, landing_shape),
        in_specs=vmem(13),
        out_specs=tuple(vmem(4)),
        scratch_shapes=[
            pltpu.VMEM(wide_shape.shape, jnp.bfloat16),
            pltpu.VMEM(wide_shape.shape, jnp.bfloat16),
            pltpu.VMEM((channels, cells), jnp.float32),
            pltpu.VMEM((channels, cells), jnp.float32),
            taps_scratch,
            taps_scratch,
            *plan.wide_scratch(),
            *plan.wide_scratch(),
            *plan.sum_scratch(),
            *plan.sum_scratch(),
            *plan.weight_scratch(depths[0]),
            *plan.weight_scratch(depths[1]),
            *plan.mirror_scratch(turned),
            pltpu.VMEM((9 * channels, channels), jnp.float32),
        ],
        compiler_params=pltpu.CompilerParams(
            collective_id=1, has_side_effects=True, vmem_limit_bytes=42 * 2**20
        ),
        cost_estimate=pl.CostEstimate(
            flops=20 * flops, bytes_accessed=200 * 2**20, transcendentals=0
        ),
    )(
        x, wide_x, wide_h, n_first, n_second, inv_first, inv_second, sym, hidden,
        conv_first, conv_second, w_head.T, turned,
    )
    logit_mirror = mirror_unpack(arrived, bins, height).astype(jnp.float32)
    logits = (0.5 * (raw_logits + logit_mirror)).astype(jnp.bfloat16)
    inverse_len = 1.0 / length

    def kernel_grad(table):
        part = table[:folded] * inverse_len
        part = jnp.concatenate([part[:, :channels], part[:, channels : 2 * channels]], axis=0)
        part = part.reshape(3, 3, channels, channels).transpose(1, 0, 3, 2)
        return part.reshape(9, channels, channels)

    sum_first, sum_second = sum_first.reshape(-1, 128), sum_second.reshape(-1, 128)
    head = sum_second[folded : folded + bins] * inverse_len
    return (
        logits,
        grad_x.reshape(channels, height, lanes),
        kernel_grad(sum_first),
        kernel_grad(sum_second),
        head[:, :channels],
        head[:, channels],
    )


def solution(mesh):
    placed = (P(None, "col", "row"), P(), P(), P(), P(), P(None, "col", "row"))
    return jax.shard_map(
        on_device,
        mesh=mesh,
        in_specs=placed,
        out_specs=(P(None, "col", "row"), P(None, "col", "row"), P(), P(), P(), P()),
        check_vma=False,
    )
```

```python
import functools

import jax
import jax.numpy as jnp
from jax import lax
from jax.experimental import pallas as pl
from jax.experimental.pallas import tpu as pltpu
from jax.sharding import PartitionSpec as P

DILATION_STEP = 16


epsilon = 1e-05


def elu_apply(value_entries):
    return jnp.where(
        value_entries > 0, value_entries, jnp.exp(jnp.minimum(value_entries, 0.0)) - 1.0
    )


def elu_slope(value_entries):
    return jnp.where(value_entries > 0, 1.0, jnp.exp(jnp.minimum(value_entries, 0.0)))


def greet(axis, count):
    me = lax.axis_index(axis)
    barrier = pltpu.get_barrier_semaphore()
    for step in range(1, count):
        pl.semaphore_signal(
            barrier,
            inc=1,
            device_id={axis: lax.rem(me + step, count)},
            device_id_type=pl.DeviceIdType.MESH,
        )


def share(axis, count, source, landing, send_sem, recv_sem):
    me = lax.axis_index(axis)
    copies = []
    for step in range(1, count):
        target = lax.rem(me + step, count)
        copy = pltpu.make_async_remote_copy(
            src_ref=source(target),
            dst_ref=landing.at[me],
            send_sem=send_sem.at[step - 1],
            recv_sem=recv_sem.at[step - 1],
            device_id={axis: target},
            device_id_type=pl.DeviceIdType.MESH,
        )
        copy.start()
        copies.append(copy)
    return copies


def finish(copies):
    for copy in copies:
        copy.wait()


def in_order(ref, count):
    total = ref[0]
    for index in range(1, count):
        total = total + ref[index]
    return total


def mirror_pack(tensor, rows):
    planes, edge, lanes = tensor.shape
    each = -(-planes // rows)
    halves = lanes // edge
    padded = jnp.pad(tensor, ((0, each * rows - planes), (0, 0), (0, 0)))
    turned = padded.reshape(rows, each, edge, lanes).transpose(0, 1, 3, 2)
    fold, deep = 128 // edge, edge * edge // 128
    pieces = []
    for half in range(halves):
        first = half * edge
        parts = [
            turned[:, :, first + u * deep : first + (u + 1) * deep] for u in range(fold)
        ]
        pieces.append(jnp.concatenate(parts, axis=3))
    return jnp.stack(pieces, axis=1)


def mirror_unpack(arrived, planes, edge):
    rows, halves, each = arrived.shape[:3]
    fold = 128 // edge
    sides = []
    for half in range(halves):
        parts = [arrived[:, half, :, :, u * edge : (u + 1) * edge] for u in range(fold)]
        sides.append(jnp.concatenate(parts, axis=2))
    return jnp.concatenate(sides, axis=3).reshape(rows * each, edge, halves * edge)[:planes]


class Mirror:
    def __init__(self, rows, cols, source, landing, refs):
        self.rows, self.cols = rows, cols
        self.source, self.landing = source, landing
        self.first, self.second = refs[:2]
        self.sems = refs[2:]
        self.ratio = cols // rows
        self.copies = None

    def hop_one(self):
        row = lax.axis_index("row")
        self.first[row] = self.source[row]
        self.copies = share(
            "row", self.rows, lambda t: self.source.at[t], self.first, *self.sems[0:2]
        )

    def hop_two(self):
        finish(self.copies)
        col, ratio = lax.axis_index("col"), self.ratio
        self.second[col] = self.first[lax.div(col, ratio), lax.rem(col, ratio)]
        self.copies = share(
            "col",
            self.cols,
            lambda t: self.first.at[lax.div(t, ratio), lax.rem(t, ratio)],
            self.second,
            *self.sems[2:4],
        )

    def hop_three(self):
        finish(self.copies)
        row, ratio = lax.axis_index("row"), self.ratio
        self.landing[row] = self.second[pl.ds(row * ratio, ratio)]
        self.copies = share(
            "row",
            self.rows,
            lambda t: self.second.at[pl.ds(t * ratio, ratio)],
            self.landing,
            *self.sems[4:6],
        )

    def end(self):
        finish(self.copies)


class WeightSum:
    def __init__(self, rows, cols, depth, refs):
        self.rows, self.cols, self.depth = rows, cols, depth
        self.mine, self.parts, self.over_row, self.whole = refs[:4]
        self.sems = refs[4:]
        self.copies = None

    def piece(self, t):
        return self.mine.at[pl.ds(pl.multiple_of(t * self.depth, 8), self.depth)]

    def scatter(self):
        col = lax.axis_index("col")
        self.parts[col] = self.piece(col)[...]
        self.copies = share("col", self.cols, self.piece, self.parts, *self.sems[0:2])

    def across(self):
        finish(self.copies)
        row = lax.axis_index("row")
        self.over_row[row] = in_order(self.parts, self.cols)
        self.copies = share(
            "row", self.rows, lambda t: self.over_row.at[row], self.over_row, *self.sems[2:4]
        )

    def gather(self):
        finish(self.copies)
        col = lax.axis_index("col")
        self.whole[col] = in_order(self.over_row, self.rows)
        self.copies = share(
            "col", self.cols, lambda t: self.whole.at[col], self.whole, *self.sems[4:6]
        )

    def end(self):
        finish(self.copies)


def dma(count):
    return pltpu.SemaphoreType.DMA((count,))


DIRECTIONS = ((0, -1), (0, 1), (-1, 0), (1, 0), (-1, -1), (-1, 1), (1, -1), (1, 1))


def meet(rows, cols):
    row, col = lax.axis_index("row"), lax.axis_index("col")
    greet("row", rows)
    greet("col", cols)
    barrier = pltpu.get_barrier_semaphore()
    corners = [pair for pair in DIRECTIONS if pair[0] and pair[1]]
    for down, across in corners:
        pl.semaphore_signal(
            barrier,
            inc=1,
            device_id={
                "row": lax.rem(row + rows + down, rows),
                "col": lax.rem(col + cols + across, cols),
            },
            device_id_type=pl.DeviceIdType.MESH,
        )
    pl.semaphore_wait(barrier, rows + cols - 2 + len(corners))


class Plan:
    def __init__(self, channels, height, lanes, rows, cols):
        self.channels, self.height, self.lanes = channels, height, lanes
        self.rows, self.cols = rows, cols
        self.margin = DILATION_STEP * lanes
        self.cells = height * lanes
        self.group = lanes // DILATION_STEP
        self.chunk = self.group * lanes
        self.chunks = self.cells // self.chunk
        self.width = self.cells + 2 * self.margin
        self.edge = DILATION_STEP // self.group * lanes
        self.strip = self.chunks * lanes
        self.strip_width = self.strip + 2 * self.edge

    def wide_scratch(self):
        return [
            pltpu.VMEM((self.channels, self.strip), jnp.bfloat16),
            pltpu.VMEM((self.channels, self.strip), jnp.bfloat16),
            pltpu.VMEM((self.channels, self.strip_width), jnp.bfloat16),
            pltpu.VMEM((self.channels, self.strip_width), jnp.bfloat16),
            dma(8),
            dma(8),
        ]

    def sum_scratch(self):
        return [
            pltpu.VMEM((self.rows, 8, 128), jnp.float32),
            pltpu.VMEM((self.cols, 8, 128), jnp.float32),
            dma(self.rows - 1),
            dma(self.rows - 1),
            dma(self.cols - 1),
            dma(self.cols - 1),
        ]

    def line(self, index, m, offset=0):
        return pl.ds(pl.multiple_of(index * self.chunk + offset + m * self.lanes, 128), self.lanes)

    def mirror_scratch(self, packed):
        return [
            pltpu.VMEM(packed.shape, jnp.bfloat16),
            pltpu.VMEM((self.cols, *packed.shape[2:]), jnp.bfloat16),
            dma(self.rows - 1),
            dma(self.rows - 1),
            dma(self.cols - 1),
            dma(self.cols - 1),
            dma(self.rows - 1),
            dma(self.rows - 1),
        ]

    def depth(self, count):
        return -(-count // (self.cols * 8)) * 8

    def weight_scratch(self, depth):
        return [
            pltpu.VMEM((self.cols * depth, 128), jnp.float32),
            pltpu.VMEM((self.cols, depth, 128), jnp.float32),
            pltpu.VMEM((self.rows, depth, 128), jnp.float32),
            pltpu.VMEM((self.cols, depth, 128), jnp.float32),
            dma(self.cols - 1),
            dma(self.cols - 1),
            dma(self.rows - 1),
            dma(self.rows - 1),
            dma(self.cols - 1),
            dma(self.cols - 1),
        ]

    def at(self, index, offset=0, size=None):
        size = self.chunk if size is None else size
        return pl.ds(pl.multiple_of(index * size + offset, 128), size)


def clear(plan, wide, low, high):
    middle = slice(plan.channels, 2 * plan.channels)
    blank = jnp.zeros((plan.channels, plan.margin), jnp.bfloat16)
    wide[middle, : plan.margin] = blank
    wide[middle, plan.width - plan.margin :] = blank
    low[...] = jnp.zeros_like(low)
    high[...] = jnp.zeros_like(high)


def emit(plan, wide, last, first, index, make):
    n, lanes, step = plan.channels, plan.lanes, DILATION_STEP
    lane = lax.broadcasted_iota(jnp.int32, (n, lanes), 1)
    tail, lead = jnp.zeros((n, lanes), jnp.float32), jnp.zeros((n, lanes), jnp.float32)
    for m in range(plan.group):
        line = make(plan.line(index, m))
        place = plan.line(index, m, plan.margin)
        right = pltpu.roll(line, step, 1)
        left = pltpu.roll(line, lanes - step, 1)
        wide[n : 2 * n, place] = line.astype(jnp.bfloat16)
        wide[0:n, place] = right.astype(jnp.bfloat16)
        wide[2 * n : 3 * n, place] = left.astype(jnp.bfloat16)
        mine = (lane >= m * step) & (lane < (m + 1) * step)
        tail = jnp.where(mine, pltpu.roll(right, m * step, 1) if m else right, tail)
        lead = jnp.where(mine, pltpu.roll(line, m * step, 1) if m else line, lead)
    spot = plan.at(index, 0, lanes)
    last[:, spot] = tail.astype(jnp.bfloat16)
    first[:, spot] = lead.astype(jnp.bfloat16)


def halo_copies(plan, wide, last, first, low, high, send_sem, recv_sem):
    row, col = lax.axis_index("row"), lax.axis_index("col")
    n = plan.channels
    middle = slice(n, 2 * n)
    found = []
    for index, (down, across) in enumerate(DIRECTIONS):
        if down == 0:
            if across < 0:
                source = wide.at[middle, plan.margin : 2 * plan.margin]
                target = wide.at[middle, plan.width - plan.margin : plan.width]
            else:
                source = wide.at[middle, plan.cells : plan.cells + plan.margin]
                target = wide.at[middle, 0 : plan.margin]
        else:
            strip, landing = (last, low) if down > 0 else (first, high)
            if across == 0:
                source, target = strip, landing.at[:, plan.edge : plan.edge + plan.strip]
            elif across > 0:
                source = strip.at[:, plan.strip - plan.edge : plan.strip]
                target = landing.at[:, 0 : plan.edge]
            else:
                source = strip.at[:, 0 : plan.edge]
                target = landing.at[:, plan.edge + plan.strip : plan.strip_width]
        there = {
            "row": jnp.clip(row + down, 0, plan.rows - 1),
            "col": jnp.clip(col + across, 0, plan.cols - 1),
        }
        copy = pltpu.make_async_remote_copy(
            src_ref=source,
            dst_ref=target,
            send_sem=send_sem.at[index],
            recv_sem=recv_sem.at[index],
            device_id=there,
            device_id_type=pl.DeviceIdType.MESH,
        )

        def inside(r, c):
            return (r >= 0) & (r < plan.rows) & (c >= 0) & (c < plan.cols)

        found.append((copy, inside(row + down, col + across), inside(row - down, col - across)))
    return found


def halo_start(copies):
    for copy, sends, _ in copies:
        pl.when(sends)(copy.start)


def halo_wait(copies):
    for copy, sends, receives in copies:
        pl.when(receives)(copy.wait_recv)
        pl.when(sends)(copy.wait_send)


def mend(plan, wide, low, high):
    n, lanes, step = plan.channels, plan.lanes, DILATION_STEP
    lane = lax.broadcasted_iota(jnp.int32, (n, lanes), 1)

    def fill(index, fresh):
        spot = plan.at(index, 0, lanes)
        before = low[:, spot].astype(jnp.float32)
        after = high[:, spot].astype(jnp.float32)
        for m in range(plan.group):
            place = plan.line(index, m)
            if fresh:
                middle = wide[n : 2 * n, place].astype(jnp.float32)
                right = pltpu.roll(middle, step, 1)
                left = pltpu.roll(middle, lanes - step, 1)
            else:
                right = wide[0:n, place].astype(jnp.float32)
                left = wide[2 * n : 3 * n, place].astype(jnp.float32)
            enter = pltpu.roll(before, (lanes - m * step) % lanes, 1) if m else before
            back = (lanes - step - m * step) % lanes
            leave = pltpu.roll(after, back, 1) if back else after
            wide[0:n, place] = jnp.where(lane < step, enter, right).astype(jnp.bfloat16)
            wide[2 * n : 3 * n, place] = jnp.where(
                lane >= lanes - step, leave, left
            ).astype(jnp.bfloat16)

    side = plan.margin // plan.chunk

    def outer(index, carry):
        fill(index, True)
        fill(index + side + plan.chunks, True)
        return carry

    def inner(index, carry):
        fill(index + side, False)
        return carry

    lax.fori_loop(0, side, outer, 0)
    lax.fori_loop(0, plan.chunks, inner, 0)


def conv_chunk(plan, wide, weight, index):
    total = None
    for b in range(3):
        part = jnp.dot(
            weight[b],
            wide[:, plan.at(index, b * plan.margin)],
            preferred_element_type=jnp.float32,
        )
        total = part if total is None else total + part
    return total


def weight_chunk(plan, wide, gradient, index):
    windows = [wide[:, plan.at(index, b * plan.margin)] for b in range(3)]
    return lax.dot_general(
        jnp.concatenate(windows, axis=0),
        gradient,
        (((1,), (1,)), ((), ())),
        preferred_element_type=jnp.float32,
    )


def total_sums(plan, pair, over_row, over_col, row_out, row_in, col_out, col_in):
    row, col = lax.axis_index("row"), lax.axis_index("col")
    n = plan.channels
    lane = lax.broadcasted_iota(jnp.int32, (n, 128), 1)
    both = jnp.where(lane == 0, pair[0], jnp.where(lane == 1, pair[1], 0.0))
    square = jnp.concatenate([both, jnp.zeros((128 - n, 128), jnp.float32)], axis=0)
    over_row[row] = square.T[0:8]
    finish(share("row", plan.rows, lambda t: over_row.at[row], over_row, row_out, row_in))
    over_col[col] = in_order(over_row, plan.rows)
    finish(share("col", plan.cols, lambda t: over_col.at[col], over_col, col_out, col_in))
    summed = in_order(over_col, plan.cols)
    back = jnp.concatenate([summed, jnp.zeros((120, 128), jnp.float32)], axis=0).T
    return back[0:n, 0:1], back[0:n, 1:2]


def reduced(pair):
    return tuple(jnp.sum(part, axis=1, keepdims=True) for part in pair)


def forward_kernel(plan, cell_count, *refs):
    x, k_first, k_second, w_head, bias, turned = refs[:6]
    wide_x, wide_h, n_first, n_second, raw, hidden, inv_first, inv_second, landing = refs[6:15]
    act, w_first, w_second = refs[15:18]
    ends_x, ends_h = refs[18:24], refs[24:30]
    sums_first, sums_second = refs[30:36], refs[36:42]
    mirror = Mirror(plan.rows, plan.cols, turned, landing, refs[42:50])
    n = plan.channels
    zero = jnp.zeros((n, plan.lanes), jnp.float32)
    clear(plan, wide_x, ends_x[2], ends_x[3])
    clear(plan, wide_h, ends_h[2], ends_h[3])
    meet(plan.rows, plan.cols)
    build_taps(k_first, w_first, False)
    build_taps(k_second, w_second, False)

    def load(index, carry):
        emit(
            plan, wide_x, ends_x[0], ends_x[1], index, lambda at: x[:, at].astype(jnp.float32)
        )
        return carry

    lax.fori_loop(0, plan.chunks, load, 0)
    copies = halo_copies(plan, wide_x, *ends_x)
    halo_start(copies)
    halo_wait(copies)
    mirror.hop_one()
    mend(plan, wide_x, ends_x[2], ends_x[3])

    def convolve(wide, weight):
        def body(index, carry):
            part = conv_chunk(plan, wide, weight, index)
            act[:, plan.at(index)] = part
            total, square = carry
            for m in range(plan.group):
                line = part[:, m * plan.lanes : (m + 1) * plan.lanes]
                total, square = total + line, square + line * line
            return total, square

        return reduced(lax.fori_loop(0, plan.chunks, body, (zero, zero)))

    def moments(pair, scratch, kept):
        totals, squares = total_sums(plan, pair, *scratch)
        average = totals / cell_count
        inverse = lax.rsqrt(squares / cell_count - average * average + epsilon)
        kept[...] = jnp.broadcast_to(inverse, kept.shape)
        return average, inverse

    average, inverse = moments(convolve(wide_x, w_first), sums_first, inv_first)
    mirror.hop_two()

    def middle(index, carry):
        def make(at):
            normed = (act[:, at] - average) * inverse
            n_first[:, at] = normed
            return elu_apply(normed)

        emit(plan, wide_h, ends_h[0], ends_h[1], index, make)
        return carry

    lax.fori_loop(0, plan.chunks, middle, 0)
    copies = halo_copies(plan, wide_h, *ends_h)
    halo_start(copies)
    halo_wait(copies)
    mend(plan, wide_h, ends_h[2], ends_h[3])
    mirror.hop_three()
    average_2, inverse_2 = moments(convolve(wide_h, w_second), sums_second, inv_second)

    def tail(index, carry):
        place = plan.at(index)
        for m in range(plan.group):
            at = plan.line(index, m)
            normed = (act[:, at] - average_2) * inverse_2
            n_second[:, at] = normed
            out = elu_apply(normed + x[:, at].astype(jnp.float32))
            hidden[:, at] = out.astype(jnp.bfloat16)
        raw[:, place] = (
            jnp.dot(w_head[...], hidden[:, place], preferred_element_type=jnp.float32) + bias[:, 0:1]
        )
        return carry

    lax.fori_loop(0, plan.chunks, tail, 0)
    mirror.end()


def backward_kernel(plan, cell_count, depths, *refs):
    (x, wide_x, wide_h, n_first, n_second, inv_first, inv_second) = refs[:7]
    sym, hidden, k_first, k_second, w_head, turned = refs[7:13]
    grad_x, sum_first, sum_second, landing = refs[13:17]
    wide_2, wide_1, slope_grad, inner_grad, w_first, w_second = refs[17:23]
    ends_2, ends_1 = refs[23:29], refs[29:35]
    sums_2, sums_1 = refs[35:41], refs[41:47]
    late = WeightSum(plan.rows, plan.cols, depths[0], refs[47:57])
    early = WeightSum(plan.rows, plan.cols, depths[1], refs[57:67])
    mirror = Mirror(plan.rows, plan.cols, turned, landing, refs[67:75])
    piled = refs[75]
    n, bins = plan.channels, sym.shape[0]
    folded = 9 * n // 2
    zero = jnp.zeros((n, plan.lanes), jnp.float32)
    clear(plan, wide_2, ends_2[2], ends_2[3])
    clear(plan, wide_1, ends_1[2], ends_1[3])
    late.mine[...] = jnp.zeros_like(late.mine)
    early.mine[...] = jnp.zeros_like(early.mine)
    meet(plan.rows, plan.cols)
    mirror.hop_one()
    build_taps(k_first, w_first, True)
    build_taps(k_second, w_second, True)
    head_at = folded

    def start(index, carry):
        place = plan.at(index)
        sym_part = sym[:, place]
        part = jnp.dot(w_head[...], sym_part, preferred_element_type=jnp.float32)
        total, cross = carry
        for m in range(plan.group):
            at = plan.line(index, m)
            normed = n_second[:, at]
            line = part[:, m * plan.lanes : (m + 1) * plan.lanes]
            line = line * elu_slope(normed + x[:, at].astype(jnp.float32))
            slope_grad[:, at] = line
            total, cross = total + line, cross + line * normed
        early.mine[head_at : head_at + bins, 0:n] += lax.dot_general(
            sym_part, hidden[:, place], (((1,), (1,)), ((), ())),
            preferred_element_type=jnp.float32,
        )
        early.mine[head_at : head_at + bins, n:] += jnp.broadcast_to(
            jnp.sum(sym_part.astype(jnp.float32), axis=1, keepdims=True), (bins, 128 - n)
        )
        return total, cross

    pair = reduced(lax.fori_loop(0, plan.chunks, start, (zero, zero)))

    def step_back(pair, scratch, source, normed, inverse_ref, wide, ends, beside):
        first_sum, second_sum = total_sums(plan, pair, *scratch)
        beside()
        first_mean, second_mean = first_sum / cell_count, second_sum / cell_count
        inverse = inverse_ref[:, 0:1]

        def body(index, carry):
            def make(at):
                return inverse * (source[:, at] - first_mean - normed[:, at] * second_mean)

            emit(plan, wide, ends[0], ends[1], index, make)
            return carry

        lax.fori_loop(0, plan.chunks, body, 0)
        copies = halo_copies(plan, wide, *ends)
        halo_start(copies)
        return copies

    def weigh(wide, against, table):
        def body(index, carry):
            gradient = wide[n : 2 * n, plan.at(index, plan.margin)]
            piled[...] += weight_chunk(plan, against, gradient, index)
            return carry

        piled[...] = jnp.zeros_like(piled)
        lax.fori_loop(0, plan.chunks, body, 0)
        table.mine[0:folded, :] = jnp.concatenate([piled[0:folded], piled[folded:]], axis=1)

    copies = step_back(
        pair, sums_2, slope_grad, n_second, inv_second, wide_2, ends_2, mirror.hop_two
    )
    weigh(wide_2, wide_h, early)
    halo_wait(copies)
    mend(plan, wide_2, ends_2[2], ends_2[3])
    mirror.hop_three()
    early.scatter()

    def through(index, carry):
        part = conv_chunk(plan, wide_2, w_second, index)
        total, cross = carry
        for m in range(plan.group):
            at = plan.line(index, m)
            normed = n_first[:, at]
            line = part[:, m * plan.lanes : (m + 1) * plan.lanes] * elu_slope(normed)
            inner_grad[:, at] = line
            total, cross = total + line, cross + line * normed
        return total, cross

    pair = reduced(lax.fori_loop(0, plan.chunks, through, (zero, zero)))
    early.across()
    copies = step_back(
        pair, sums_1, inner_grad, n_first, inv_first, wide_1, ends_1, early.gather
    )
    weigh(wide_1, wide_x, late)
    halo_wait(copies)
    late.scatter()
    mend(plan, wide_1, ends_1[2], ends_1[3])

    def last(index, carry):
        place = plan.at(index)
        part = conv_chunk(plan, wide_1, w_first, index) + slope_grad[:, place]
        grad_x[:, place] = part.astype(jnp.bfloat16)
        return carry

    half = plan.chunks // 2
    lax.fori_loop(0, half, last, 0)
    late.across()
    lax.fori_loop(half, plan.chunks, last, 0)
    late.gather()
    early.end()
    mirror.end()
    sum_second[...] = early.whole[...]
    late.end()
    sum_first[...] = late.whole[...]


def vmem(count):
    return [pl.BlockSpec(memory_space=pltpu.VMEM)] * count


def build_taps(kernel, table, adjoint):
    for b in range(3):
        parts = []
        for a in range(3):
            if adjoint:
                part = kernel[3 * (2 - a) + 2 - b].astype(jnp.float32).T
            else:
                part = kernel[3 * a + b].astype(jnp.float32)
            parts.append(part)
        table[b] = jnp.concatenate(parts, axis=1).astype(jnp.bfloat16)


def on_device(features, conv_first, conv_second, head_weight, head_bias, cotangent):
    channels, height, lanes = features.shape
    rows, cols = lax.axis_size("row"), lax.axis_size("col")
    length = height * cols
    cell_count = float(length * length)
    bins = head_weight.shape[0]
    padded = -(-bins // 16) * 16
    plan = Plan(channels, height, lanes, rows, cols)
    cells, width = plan.cells, plan.width
    x = features.reshape(channels, cells)
    w_head = jnp.pad(head_weight, ((0, padded - bins), (0, 0)))
    bias = jnp.broadcast_to(jnp.pad(head_bias, (0, padded - bins))[:, None], (padded, 128))
    wide_shape = jax.ShapeDtypeStruct((3 * channels, width), jnp.bfloat16)
    full_shape = jax.ShapeDtypeStruct((channels, cells), jnp.float32)
    short_shape = jax.ShapeDtypeStruct((channels, cells), jnp.bfloat16)
    inverse_shape = jax.ShapeDtypeStruct((channels, 128), jnp.float32)
    flops = 2 * 9 * channels * channels * cells
    turned = mirror_pack(cotangent, rows)
    landing_shape = jax.ShapeDtypeStruct(turned.shape, jnp.bfloat16)
    taps_scratch = pltpu.VMEM((3, channels, 3 * channels), jnp.bfloat16)
    wide_x, wide_h, n_first, n_second, raw, hidden, inv_first, inv_second, arrived = pl.pallas_call(
        functools.partial(forward_kernel, plan, cell_count),
        out_shape=(
            wide_shape,
            wide_shape,
            full_shape,
            full_shape,
            jax.ShapeDtypeStruct((padded, cells), jnp.float32),
            short_shape,
            inverse_shape,
            inverse_shape,
            landing_shape,
        ),
        in_specs=vmem(6),
        out_specs=tuple(vmem(9)),
        scratch_shapes=[
            pltpu.VMEM((channels, cells), jnp.float32),
            taps_scratch,
            taps_scratch,
            *plan.wide_scratch(),
            *plan.wide_scratch(),
            *plan.sum_scratch(),
            *plan.sum_scratch(),
            *plan.mirror_scratch(turned),
        ],
        compiler_params=pltpu.CompilerParams(
            collective_id=0, has_side_effects=True, vmem_limit_bytes=12 * 2**20
        ),
        cost_estimate=pl.CostEstimate(
            flops=20 * flops, bytes_accessed=200 * 2**20, transcendentals=0
        ),
    )(x, conv_first, conv_second, w_head, bias, turned)
    cot_mirror = mirror_unpack(arrived, bins, height)
    grad_sym = (0.5 * (cotangent.astype(jnp.float32) + cot_mirror.astype(jnp.float32))).astype(
        jnp.bfloat16
    )
    sym = jnp.pad(grad_sym.reshape(bins, cells), ((0, padded - bins), (0, 0)))
    raw_logits = raw[:bins].reshape(bins, height, lanes)
    turned = mirror_pack(raw_logits.astype(jnp.bfloat16), rows)
    folded = 9 * channels // 2
    depths = (plan.depth(folded), plan.depth(folded + padded))
    sum_shapes = [jax.ShapeDtypeStruct((cols, depth, 128), jnp.float32) for depth in depths]
    grad_x, sum_first, sum_second, arrived = pl.pallas_call(
        functools.partial(backward_kernel, plan, cell_count, depths),
        out_shape=(short_shape, *sum_shapes, landing_shape),
        in_specs=vmem(13),
        out_specs=tuple(vmem(4)),
        scratch_shapes=[
            pltpu.VMEM(wide_shape.shape, jnp.bfloat16),
            pltpu.VMEM(wide_shape.shape, jnp.bfloat16),
            pltpu.VMEM((channels, cells), jnp.float32),
            pltpu.VMEM((channels, cells), jnp.float32),
            taps_scratch,
            taps_scratch,
            *plan.wide_scratch(),
            *plan.wide_scratch(),
            *plan.sum_scratch(),
            *plan.sum_scratch(),
            *plan.weight_scratch(depths[0]),
            *plan.weight_scratch(depths[1]),
            *plan.mirror_scratch(turned),
            pltpu.VMEM((9 * channels, channels), jnp.float32),
        ],
        compiler_params=pltpu.CompilerParams(
            collective_id=1, has_side_effects=True, vmem_limit_bytes=26 * 2**20
        ),
        cost_estimate=pl.CostEstimate(
            flops=20 * flops, bytes_accessed=200 * 2**20, transcendentals=0
        ),
    )(
        x, wide_x, wide_h, n_first, n_second, inv_first, inv_second, sym, hidden,
        conv_first, conv_second, w_head.T, turned,
    )
    logit_mirror = mirror_unpack(arrived, bins, height).astype(jnp.float32)
    logits = (0.5 * (raw_logits + logit_mirror)).astype(jnp.bfloat16)
    inverse_len = 1.0 / length

    def kernel_grad(table):
        part = table[:folded] * inverse_len
        part = jnp.concatenate([part[:, :channels], part[:, channels : 2 * channels]], axis=0)
        part = part.reshape(3, 3, channels, channels).transpose(1, 0, 3, 2)
        return part.reshape(9, channels, channels)

    sum_first, sum_second = sum_first.reshape(-1, 128), sum_second.reshape(-1, 128)
    head = sum_second[folded : folded + bins] * inverse_len
    return (
        logits,
        grad_x.reshape(channels, height, lanes),
        kernel_grad(sum_first),
        kernel_grad(sum_second),
        head[:, :channels],
        head[:, channels],
    )


def solution(mesh):
    placed = (P(None, "col", "row"), P(), P(), P(), P(), P(None, "col", "row"))
    return jax.shard_map(
        on_device,
        mesh=mesh,
        in_specs=placed,
        out_specs=(P(None, "col", "row"), P(None, "col", "row"), P(), P(), P(), P()),
        check_vma=False,
    )
```

```python
import functools

import jax
import jax.numpy as jnp
from jax import lax
from jax.experimental import pallas as pl
from jax.experimental.pallas import tpu as pltpu
from jax.sharding import PartitionSpec as P

DILATION_STEP = 16


epsilon = 1e-05


def elu_apply(value_entries):
    return jnp.where(
        value_entries > 0, value_entries, jnp.exp(jnp.minimum(value_entries, 0.0)) - 1.0
    )


def elu_slope(value_entries):
    return jnp.where(value_entries > 0, 1.0, jnp.exp(jnp.minimum(value_entries, 0.0)))


def greet(axis, count):
    me = lax.axis_index(axis)
    barrier = pltpu.get_barrier_semaphore()
    for step in range(1, count):
        pl.semaphore_signal(
            barrier,
            inc=1,
            device_id={axis: lax.rem(me + step, count)},
            device_id_type=pl.DeviceIdType.MESH,
        )


def share(axis, count, source, landing, send_sem, recv_sem):
    me = lax.axis_index(axis)
    copies = []
    for step in range(1, count):
        target = lax.rem(me + step, count)
        copy = pltpu.make_async_remote_copy(
            src_ref=source(target),
            dst_ref=landing.at[me],
            send_sem=send_sem.at[step - 1],
            recv_sem=recv_sem.at[step - 1],
            device_id={axis: target},
            device_id_type=pl.DeviceIdType.MESH,
        )
        copy.start()
        copies.append(copy)
    return copies


def finish(copies):
    for copy in copies:
        copy.wait()


def in_order(ref, count):
    total = ref[0]
    for index in range(1, count):
        total = total + ref[index]
    return total


def mirror_pack(tensor, rows):
    planes, edge, lanes = tensor.shape
    each = -(-planes // rows)
    halves = lanes // edge
    padded = jnp.pad(tensor, ((0, each * rows - planes), (0, 0), (0, 0)))
    turned = padded.reshape(rows, each, edge, lanes).transpose(0, 1, 3, 2)
    fold, deep = 128 // edge, edge * edge // 128
    pieces = []
    for half in range(halves):
        first = half * edge
        parts = [
            turned[:, :, first + u * deep : first + (u + 1) * deep] for u in range(fold)
        ]
        pieces.append(jnp.concatenate(parts, axis=3))
    return jnp.stack(pieces, axis=1)


def mirror_unpack(arrived, planes, edge):
    rows, halves, each = arrived.shape[:3]
    fold = 128 // edge
    sides = []
    for half in range(halves):
        parts = [arrived[:, half, :, :, u * edge : (u + 1) * edge] for u in range(fold)]
        sides.append(jnp.concatenate(parts, axis=2))
    return jnp.concatenate(sides, axis=3).reshape(rows * each, edge, halves * edge)[:planes]


class Mirror:
    def __init__(self, rows, cols, source, landing, refs):
        self.rows, self.cols = rows, cols
        self.source, self.landing = source, landing
        self.first, self.second = refs[:2]
        self.sems = refs[2:]
        self.ratio = cols // rows
        self.copies = None

    def hop_one(self):
        row = lax.axis_index("row")
        self.first[row] = self.source[row]
        self.copies = share(
            "row", self.rows, lambda t: self.source.at[t], self.first, *self.sems[0:2]
        )

    def hop_two(self):
        finish(self.copies)
        col, ratio = lax.axis_index("col"), self.ratio
        self.second[col] = self.first[lax.div(col, ratio), lax.rem(col, ratio)]
        self.copies = share(
            "col",
            self.cols,
            lambda t: self.first.at[lax.div(t, ratio), lax.rem(t, ratio)],
            self.second,
            *self.sems[2:4],
        )

    def hop_three(self):
        finish(self.copies)
        row, ratio = lax.axis_index("row"), self.ratio
        self.landing[row] = self.second[pl.ds(row * ratio, ratio)]
        self.copies = share(
            "row",
            self.rows,
            lambda t: self.second.at[pl.ds(t * ratio, ratio)],
            self.landing,
            *self.sems[4:6],
        )

    def end(self):
        finish(self.copies)


class WeightSum:
    def __init__(self, rows, cols, depth, refs):
        self.rows, self.cols, self.depth = rows, cols, depth
        self.mine, self.parts, self.over_row, self.whole = refs[:4]
        self.sems = refs[4:]
        self.copies = None

    def piece(self, t):
        return self.mine.at[pl.ds(pl.multiple_of(t * self.depth, 8), self.depth)]

    def scatter(self):
        col = lax.axis_index("col")
        self.parts[col] = self.piece(col)[...]
        self.copies = share("col", self.cols, self.piece, self.parts, *self.sems[0:2])

    def across(self):
        finish(self.copies)
        row = lax.axis_index("row")
        self.over_row[row] = in_order(self.parts, self.cols)
        self.copies = share(
            "row", self.rows, lambda t: self.over_row.at[row], self.over_row, *self.sems[2:4]
        )

    def gather(self):
        finish(self.copies)
        col = lax.axis_index("col")
        self.whole[col] = in_order(self.over_row, self.rows)
        self.copies = share(
            "col", self.cols, lambda t: self.whole.at[col], self.whole, *self.sems[4:6]
        )

    def end(self):
        finish(self.copies)


def dma(count):
    return pltpu.SemaphoreType.DMA((count,))


DIRECTIONS = ((0, -1), (0, 1), (-1, 0), (1, 0), (-1, -1), (-1, 1), (1, -1), (1, 1))


def meet(rows, cols):
    row, col = lax.axis_index("row"), lax.axis_index("col")
    greet("row", rows)
    greet("col", cols)
    barrier = pltpu.get_barrier_semaphore()
    corners = [pair for pair in DIRECTIONS if pair[0] and pair[1]]
    for down, across in corners:
        pl.semaphore_signal(
            barrier,
            inc=1,
            device_id={
                "row": lax.rem(row + rows + down, rows),
                "col": lax.rem(col + cols + across, cols),
            },
            device_id_type=pl.DeviceIdType.MESH,
        )
    pl.semaphore_wait(barrier, rows + cols - 2 + len(corners))


class Plan:
    def __init__(self, channels, height, lanes, rows, cols):
        self.channels, self.height, self.lanes = channels, height, lanes
        self.rows, self.cols = rows, cols
        self.margin = DILATION_STEP * lanes
        self.cells = height * lanes
        self.group = lanes // DILATION_STEP
        self.chunk = self.group * lanes
        self.chunks = self.cells // self.chunk
        self.width = self.cells + 2 * self.margin
        self.edge = DILATION_STEP // self.group * lanes
        self.strip = self.chunks * lanes
        self.strip_width = self.strip + 2 * self.edge

    def wide_scratch(self):
        return [
            pltpu.VMEM((self.channels, self.strip), jnp.bfloat16),
            pltpu.VMEM((self.channels, self.strip), jnp.bfloat16),
            pltpu.VMEM((self.channels, self.strip_width), jnp.bfloat16),
            pltpu.VMEM((self.channels, self.strip_width), jnp.bfloat16),
            dma(8),
            dma(8),
        ]

    def sum_scratch(self):
        return [
            pltpu.VMEM((self.rows, 8, 128), jnp.float32),
            pltpu.VMEM((self.cols, 8, 128), jnp.float32),
            dma(self.rows - 1),
            dma(self.rows - 1),
            dma(self.cols - 1),
            dma(self.cols - 1),
        ]

    def mirror_scratch(self, packed):
        return [
            pltpu.VMEM(packed.shape, jnp.bfloat16),
            pltpu.VMEM((self.cols, *packed.shape[2:]), jnp.bfloat16),
            dma(self.rows - 1),
            dma(self.rows - 1),
            dma(self.cols - 1),
            dma(self.cols - 1),
            dma(self.rows - 1),
            dma(self.rows - 1),
        ]

    def depth(self, count):
        return -(-count // (self.cols * 8)) * 8

    def weight_scratch(self, depth):
        return [
            pltpu.VMEM((self.cols * depth, 128), jnp.float32),
            pltpu.VMEM((self.cols, depth, 128), jnp.float32),
            pltpu.VMEM((self.rows, depth, 128), jnp.float32),
            pltpu.VMEM((self.cols, depth, 128), jnp.float32),
            dma(self.cols - 1),
            dma(self.cols - 1),
            dma(self.rows - 1),
            dma(self.rows - 1),
            dma(self.cols - 1),
            dma(self.cols - 1),
        ]

    def at(self, index, offset=0, size=None):
        size = self.chunk if size is None else size
        return pl.ds(pl.multiple_of(index * size + offset, 128), size)


def clear(plan, wide, low, high):
    middle = slice(plan.channels, 2 * plan.channels)
    blank = jnp.zeros((plan.channels, plan.margin), jnp.bfloat16)
    wide[middle, : plan.margin] = blank
    wide[middle, plan.width - plan.margin :] = blank
    low[...] = jnp.zeros_like(low)
    high[...] = jnp.zeros_like(high)


def emit(plan, wide, last, first, index, values):
    n, lanes, step = plan.channels, plan.lanes, DILATION_STEP
    place = plan.at(index, plan.margin)
    lane = lax.broadcasted_iota(jnp.int32, (n, lanes), 1)
    wide[n : 2 * n, place] = values.astype(jnp.bfloat16)
    later, sooner = [], []
    tail, lead = jnp.zeros((n, lanes), jnp.float32), jnp.zeros((n, lanes), jnp.float32)
    for m in range(plan.group):
        line = values[:, m * lanes : (m + 1) * lanes]
        right = pltpu.roll(line, step, 1)
        left = pltpu.roll(line, lanes - step, 1)
        later.append(right.astype(jnp.bfloat16))
        sooner.append(left.astype(jnp.bfloat16))
        mine = (lane >= m * step) & (lane < (m + 1) * step)
        tail = jnp.where(mine, pltpu.roll(right, m * step, 1) if m else right, tail)
        lead = jnp.where(mine, pltpu.roll(line, m * step, 1) if m else line, lead)
    wide[0:n, place] = jnp.concatenate(later, axis=1)
    wide[2 * n : 3 * n, place] = jnp.concatenate(sooner, axis=1)
    spot = plan.at(index, 0, lanes)
    last[:, spot] = tail.astype(jnp.bfloat16)
    first[:, spot] = lead.astype(jnp.bfloat16)


def halo_copies(plan, wide, last, first, low, high, send_sem, recv_sem):
    row, col = lax.axis_index("row"), lax.axis_index("col")
    n = plan.channels
    middle = slice(n, 2 * n)
    found = []
    for index, (down, across) in enumerate(DIRECTIONS):
        if down == 0:
            if across < 0:
                source = wide.at[middle, plan.margin : 2 * plan.margin]
                target = wide.at[middle, plan.width - plan.margin : plan.width]
            else:
                source = wide.at[middle, plan.cells : plan.cells + plan.margin]
                target = wide.at[middle, 0 : plan.margin]
        else:
            strip, landing = (last, low) if down > 0 else (first, high)
            if across == 0:
                source, target = strip, landing.at[:, plan.edge : plan.edge + plan.strip]
            elif across > 0:
                source = strip.at[:, plan.strip - plan.edge : plan.strip]
                target = landing.at[:, 0 : plan.edge]
            else:
                source = strip.at[:, 0 : plan.edge]
                target = landing.at[:, plan.edge + plan.strip : plan.strip_width]
        there = {
            "row": jnp.clip(row + down, 0, plan.rows - 1),
            "col": jnp.clip(col + across, 0, plan.cols - 1),
        }
        copy = pltpu.make_async_remote_copy(
            src_ref=source,
            dst_ref=target,
            send_sem=send_sem.at[index],
            recv_sem=recv_sem.at[index],
            device_id=there,
            device_id_type=pl.DeviceIdType.MESH,
        )

        def inside(r, c):
            return (r >= 0) & (r < plan.rows) & (c >= 0) & (c < plan.cols)

        found.append((copy, inside(row + down, col + across), inside(row - down, col - across)))
    return found


def halo_start(copies):
    for copy, sends, _ in copies:
        pl.when(sends)(copy.start)


def halo_wait(copies):
    for copy, sends, receives in copies:
        pl.when(receives)(copy.wait_recv)
        pl.when(sends)(copy.wait_send)


def mend(plan, wide, low, high):
    n, lanes, step = plan.channels, plan.lanes, DILATION_STEP
    lane = lax.broadcasted_iota(jnp.int32, (n, lanes), 1)

    def fill(index, fresh):
        place = plan.at(index)
        spot = plan.at(index, 0, lanes)
        before = low[:, spot].astype(jnp.float32)
        after = high[:, spot].astype(jnp.float32)
        middle = wide[n : 2 * n, place].astype(jnp.float32) if fresh else None
        old_later = None if fresh else wide[0:n, place].astype(jnp.float32)
        old_sooner = None if fresh else wide[2 * n : 3 * n, place].astype(jnp.float32)
        later, sooner = [], []
        for m in range(plan.group):
            line = slice(m * lanes, (m + 1) * lanes)
            if fresh:
                right = pltpu.roll(middle[:, line], step, 1)
                left = pltpu.roll(middle[:, line], lanes - step, 1)
            else:
                right, left = old_later[:, line], old_sooner[:, line]
            enter = pltpu.roll(before, (lanes - m * step) % lanes, 1) if m else before
            back = (lanes - step - m * step) % lanes
            leave = pltpu.roll(after, back, 1) if back else after
            later.append(jnp.where(lane < step, enter, right).astype(jnp.bfloat16))
            sooner.append(jnp.where(lane >= lanes - step, leave, left).astype(jnp.bfloat16))
        wide[0:n, place] = jnp.concatenate(later, axis=1)
        wide[2 * n : 3 * n, place] = jnp.concatenate(sooner, axis=1)

    side = plan.margin // plan.chunk

    def outer(index, carry):
        fill(index, True)
        fill(index + side + plan.chunks, True)
        return carry

    def inner(index, carry):
        fill(index + side, False)
        return carry

    lax.fori_loop(0, side, outer, 0)
    lax.fori_loop(0, plan.chunks, inner, 0)


def conv_chunk(plan, wide, weight, index):
    total = None
    for b in range(3):
        part = jnp.dot(
            weight[b],
            wide[:, plan.at(index, b * plan.margin)],
            preferred_element_type=jnp.float32,
        )
        total = part if total is None else total + part
    return total


def weight_chunk(plan, wide, gradient, index):
    windows = [wide[:, plan.at(index, b * plan.margin)] for b in range(3)]
    return lax.dot_general(
        jnp.concatenate(windows, axis=0),
        gradient,
        (((1,), (1,)), ((), ())),
        preferred_element_type=jnp.float32,
    )


def total_sums(plan, pair, over_row, over_col, row_out, row_in, col_out, col_in):
    row, col = lax.axis_index("row"), lax.axis_index("col")
    n = plan.channels
    lane = lax.broadcasted_iota(jnp.int32, (n, 128), 1)
    both = jnp.where(lane == 0, pair[0], jnp.where(lane == 1, pair[1], 0.0))
    square = jnp.concatenate([both, jnp.zeros((128 - n, 128), jnp.float32)], axis=0)
    over_row[row] = square.T[0:8]
    finish(share("row", plan.rows, lambda t: over_row.at[row], over_row, row_out, row_in))
    over_col[col] = in_order(over_row, plan.rows)
    finish(share("col", plan.cols, lambda t: over_col.at[col], over_col, col_out, col_in))
    summed = in_order(over_col, plan.cols)
    back = jnp.concatenate([summed, jnp.zeros((120, 128), jnp.float32)], axis=0).T
    return back[0:n, 0:1], back[0:n, 1:2]


def pair_of(first, second):
    return jnp.sum(first, axis=1, keepdims=True), jnp.sum(second, axis=1, keepdims=True)


def forward_kernel(plan, cell_count, *refs):
    x, k_first, k_second, w_head, bias, turned = refs[:6]
    kept_x, kept_h, kept_n, n_second, raw, hidden, inv_first, inv_second, landing = refs[6:15]
    wide_x, wide_h, n_first, keep_sem = refs[50:54]
    act, w_first, w_second = refs[15:18]
    ends_x, ends_h = refs[18:24], refs[24:30]
    sums_first, sums_second = refs[30:36], refs[36:42]
    mirror = Mirror(plan.rows, plan.cols, turned, landing, refs[42:50])
    n = plan.channels
    zero = jnp.zeros((n, 1), jnp.float32)
    clear(plan, wide_x, ends_x[2], ends_x[3])
    clear(plan, wide_h, ends_h[2], ends_h[3])
    meet(plan.rows, plan.cols)
    build_taps(k_first, w_first, False)
    build_taps(k_second, w_second, False)

    def load(index, carry):
        emit(plan, wide_x, ends_x[0], ends_x[1], index, x[:, plan.at(index)].astype(jnp.float32))
        return carry

    lax.fori_loop(0, plan.chunks, load, 0)
    copies = halo_copies(plan, wide_x, *ends_x)
    halo_start(copies)
    halo_wait(copies)
    mirror.hop_one()
    mend(plan, wide_x, ends_x[2], ends_x[3])
    keep_x = pltpu.make_async_copy(wide_x, kept_x, keep_sem.at[0])
    keep_x.start()

    def convolve(wide, weight):
        def body(index, carry):
            part = conv_chunk(plan, wide, weight, index)
            act[:, plan.at(index)] = part
            found = pair_of(part, part * part)
            return carry[0] + found[0], carry[1] + found[1]

        return lax.fori_loop(0, plan.chunks, body, (zero, zero))

    def moments(pair, scratch, kept):
        totals, squares = total_sums(plan, pair, *scratch)
        average = totals / cell_count
        inverse = lax.rsqrt(squares / cell_count - average * average + epsilon)
        kept[...] = jnp.broadcast_to(inverse, kept.shape)
        return average, inverse

    average, inverse = moments(convolve(wide_x, w_first), sums_first, inv_first)
    mirror.hop_two()

    def middle(index, carry):
        normed = (act[:, plan.at(index)] - average) * inverse
        n_first[:, plan.at(index)] = normed
        emit(plan, wide_h, ends_h[0], ends_h[1], index, elu_apply(normed))
        return carry

    lax.fori_loop(0, plan.chunks, middle, 0)
    keep_n = pltpu.make_async_copy(n_first, kept_n, keep_sem.at[1])
    keep_n.start()
    copies = halo_copies(plan, wide_h, *ends_h)
    halo_start(copies)
    halo_wait(copies)
    mend(plan, wide_h, ends_h[2], ends_h[3])
    keep_h = pltpu.make_async_copy(wide_h, kept_h, keep_sem.at[2])
    keep_h.start()
    mirror.hop_three()
    average_2, inverse_2 = moments(convolve(wide_h, w_second), sums_second, inv_second)

    def tail(index, carry):
        place = plan.at(index)
        normed = (act[:, place] - average_2) * inverse_2
        n_second[:, place] = normed
        out = elu_apply(normed + x[:, place].astype(jnp.float32)).astype(jnp.bfloat16)
        hidden[:, place] = out
        raw[:, place] = (
            jnp.dot(w_head[...], out, preferred_element_type=jnp.float32) + bias[:, 0:1]
        )
        return carry

    lax.fori_loop(0, plan.chunks, tail, 0)
    finish([keep_x, keep_n, keep_h])
    mirror.end()


def backward_kernel(plan, cell_count, depths, *refs):
    (x, kept_x, kept_h, kept_n, n_second, inv_first, inv_second) = refs[:7]
    sym, hidden, k_first, k_second, w_head, turned = refs[7:13]
    grad_x, sum_first, sum_second, landing = refs[13:17]
    wide_2, wide_1, slope_grad, inner_grad, w_first, w_second = refs[17:23]
    ends_2, ends_1 = refs[23:29], refs[29:35]
    sums_2, sums_1 = refs[35:41], refs[41:47]
    late = WeightSum(plan.rows, plan.cols, depths[0], refs[47:57])
    early = WeightSum(plan.rows, plan.cols, depths[1], refs[57:67])
    mirror = Mirror(plan.rows, plan.cols, turned, landing, refs[67:75])
    piled, wide_x, wide_h, n_first, keep_sem = refs[75:80]
    fetch_x = pltpu.make_async_copy(kept_x, wide_x, keep_sem.at[0])
    fetch_n = pltpu.make_async_copy(kept_n, n_first, keep_sem.at[1])
    fetch_h = pltpu.make_async_copy(kept_h, wide_h, keep_sem.at[2])
    for fetch in (fetch_h, fetch_n, fetch_x):
        fetch.start()
    n, bins = plan.channels, sym.shape[0]
    folded = 9 * n // 2
    zero = jnp.zeros((n, 1), jnp.float32)
    clear(plan, wide_2, ends_2[2], ends_2[3])
    clear(plan, wide_1, ends_1[2], ends_1[3])
    late.mine[...] = jnp.zeros_like(late.mine)
    early.mine[...] = jnp.zeros_like(early.mine)
    meet(plan.rows, plan.cols)
    mirror.hop_one()
    build_taps(k_first, w_first, True)
    build_taps(k_second, w_second, True)
    head_at = folded

    def start(index, carry):
        place = plan.at(index)
        sym_part = sym[:, place]
        summed = n_second[:, place] + x[:, place].astype(jnp.float32)
        part = jnp.dot(w_head[...], sym_part, preferred_element_type=jnp.float32)
        part = part * elu_slope(summed)
        slope_grad[:, place] = part
        early.mine[head_at : head_at + bins, 0:n] += lax.dot_general(
            sym_part, hidden[:, place], (((1,), (1,)), ((), ())),
            preferred_element_type=jnp.float32,
        )
        early.mine[head_at : head_at + bins, n:] += jnp.broadcast_to(
            jnp.sum(sym_part.astype(jnp.float32), axis=1, keepdims=True), (bins, 128 - n)
        )
        found = pair_of(part, part * n_second[:, place])
        return carry[0] + found[0], carry[1] + found[1]

    pair = lax.fori_loop(0, plan.chunks, start, (zero, zero))

    def step_back(pair, scratch, source, normed, inverse_ref, wide, ends, beside):
        first_sum, second_sum = total_sums(plan, pair, *scratch)
        beside()
        first_mean, second_mean = first_sum / cell_count, second_sum / cell_count
        inverse = inverse_ref[:, 0:1]

        def body(index, carry):
            place = plan.at(index)
            value = inverse * (source[:, place] - first_mean - normed[:, place] * second_mean)
            emit(plan, wide, ends[0], ends[1], index, value)
            return carry

        lax.fori_loop(0, plan.chunks, body, 0)
        copies = halo_copies(plan, wide, *ends)
        halo_start(copies)
        return copies

    def weigh(wide, against, table):
        def body(index, carry):
            gradient = wide[n : 2 * n, plan.at(index, plan.margin)]
            piled[...] += weight_chunk(plan, against, gradient, index)
            return carry

        piled[...] = jnp.zeros_like(piled)
        lax.fori_loop(0, plan.chunks, body, 0)
        table.mine[0:folded, :] = jnp.concatenate([piled[0:folded], piled[folded:]], axis=1)

    copies = step_back(
        pair, sums_2, slope_grad, n_second, inv_second, wide_2, ends_2, mirror.hop_two
    )
    fetch_h.wait()
    weigh(wide_2, wide_h, early)
    halo_wait(copies)
    mend(plan, wide_2, ends_2[2], ends_2[3])
    mirror.hop_three()
    early.scatter()

    fetch_n.wait()

    def through(index, carry):
        place = plan.at(index)
        normed = n_first[:, place]
        part = conv_chunk(plan, wide_2, w_second, index) * elu_slope(normed)
        inner_grad[:, place] = part
        found = pair_of(part, part * normed)
        return carry[0] + found[0], carry[1] + found[1]

    pair = lax.fori_loop(0, plan.chunks, through, (zero, zero))
    early.across()
    copies = step_back(
        pair, sums_1, inner_grad, n_first, inv_first, wide_1, ends_1, early.gather
    )
    fetch_x.wait()
    weigh(wide_1, wide_x, late)
    halo_wait(copies)
    late.scatter()
    mend(plan, wide_1, ends_1[2], ends_1[3])

    def last(index, carry):
        place = plan.at(index)
        part = conv_chunk(plan, wide_1, w_first, index) + slope_grad[:, place]
        grad_x[:, place] = part.astype(jnp.bfloat16)
        return carry

    half = plan.chunks // 2
    lax.fori_loop(0, half, last, 0)
    late.across()
    lax.fori_loop(half, plan.chunks, last, 0)
    late.gather()
    early.end()
    mirror.end()
    sum_second[...] = early.whole[...]
    late.end()
    sum_first[...] = late.whole[...]


def vmem(count):
    return [pl.BlockSpec(memory_space=pltpu.VMEM)] * count


def build_taps(kernel, table, adjoint):
    for b in range(3):
        parts = []
        for a in range(3):
            if adjoint:
                part = kernel[3 * (2 - a) + 2 - b].astype(jnp.float32).T
            else:
                part = kernel[3 * a + b].astype(jnp.float32)
            parts.append(part)
        table[b] = jnp.concatenate(parts, axis=1).astype(jnp.bfloat16)


def on_device(features, conv_first, conv_second, head_weight, head_bias, cotangent):
    channels, height, lanes = features.shape
    rows, cols = lax.axis_size("row"), lax.axis_size("col")
    length = height * cols
    cell_count = float(length * length)
    bins = head_weight.shape[0]
    padded = -(-bins // 16) * 16
    plan = Plan(channels, height, lanes, rows, cols)
    cells, width = plan.cells, plan.width
    x = features.reshape(channels, cells)
    w_head = jnp.pad(head_weight, ((0, padded - bins), (0, 0)))
    bias = jnp.broadcast_to(jnp.pad(head_bias, (0, padded - bins))[:, None], (padded, 128))
    wide_shape = jax.ShapeDtypeStruct((3 * channels, width), jnp.bfloat16)
    full_shape = jax.ShapeDtypeStruct((channels, cells), jnp.float32)
    short_shape = jax.ShapeDtypeStruct((channels, cells), jnp.bfloat16)
    inverse_shape = jax.ShapeDtypeStruct((channels, 128), jnp.float32)
    flops = 2 * 9 * channels * channels * cells
    turned = mirror_pack(cotangent, rows)
    landing_shape = jax.ShapeDtypeStruct(turned.shape, jnp.bfloat16)
    kept_scratch = [
        pltpu.VMEM((3 * channels, width), jnp.bfloat16),
        pltpu.VMEM((3 * channels, width), jnp.bfloat16),
        pltpu.VMEM((channels, cells), jnp.float32),
        dma(3),
    ]
    outside = [pl.BlockSpec(memory_space=pl.ANY)] * 3
    taps_scratch = pltpu.VMEM((3, channels, 3 * channels), jnp.bfloat16)
    wide_x, wide_h, n_first, n_second, raw, hidden, inv_first, inv_second, arrived = pl.pallas_call(
        functools.partial(forward_kernel, plan, cell_count),
        out_shape=(
            wide_shape,
            wide_shape,
            full_shape,
            full_shape,
            jax.ShapeDtypeStruct((padded, cells), jnp.float32),
            short_shape,
            inverse_shape,
            inverse_shape,
            landing_shape,
        ),
        in_specs=vmem(6),
        out_specs=(*outside, *vmem(6)),
        scratch_shapes=[
            pltpu.VMEM((channels, cells), jnp.float32),
            taps_scratch,
            taps_scratch,
            *plan.wide_scratch(),
            *plan.wide_scratch(),
            *plan.sum_scratch(),
            *plan.sum_scratch(),
            *plan.mirror_scratch(turned),
            *kept_scratch,
        ],
        compiler_params=pltpu.CompilerParams(
            collective_id=0, has_side_effects=True, vmem_limit_bytes=32 * 2**20
        ),
        cost_estimate=pl.CostEstimate(
            flops=20 * flops, bytes_accessed=200 * 2**20, transcendentals=0
        ),
    )(x, conv_first, conv_second, w_head, bias, turned)
    cot_mirror = mirror_unpack(arrived, bins, height)
    grad_sym = (0.5 * (cotangent.astype(jnp.float32) + cot_mirror.astype(jnp.float32))).astype(
        jnp.bfloat16
    )
    sym = jnp.pad(grad_sym.reshape(bins, cells), ((0, padded - bins), (0, 0)))
    raw_logits = raw[:bins].reshape(bins, height, lanes)
    turned = mirror_pack(raw_logits.astype(jnp.bfloat16), rows)
    folded = 9 * channels // 2
    depths = (plan.depth(folded), plan.depth(folded + padded))
    sum_shapes = [jax.ShapeDtypeStruct((cols, depth, 128), jnp.float32) for depth in depths]
    grad_x, sum_first, sum_second, arrived = pl.pallas_call(
        functools.partial(backward_kernel, plan, cell_count, depths),
        out_shape=(short_shape, *sum_shapes, landing_shape),
        in_specs=[*vmem(1), *outside, *vmem(9)],
        out_specs=tuple(vmem(4)),
        scratch_shapes=[
            pltpu.VMEM(wide_shape.shape, jnp.bfloat16),
            pltpu.VMEM(wide_shape.shape, jnp.bfloat16),
            pltpu.VMEM((channels, cells), jnp.float32),
            pltpu.VMEM((channels, cells), jnp.float32),
            taps_scratch,
            taps_scratch,
            *plan.wide_scratch(),
            *plan.wide_scratch(),
            *plan.sum_scratch(),
            *plan.sum_scratch(),
            *plan.weight_scratch(depths[0]),
            *plan.weight_scratch(depths[1]),
            *plan.mirror_scratch(turned),
            pltpu.VMEM((9 * channels, channels), jnp.float32),
            *kept_scratch,
        ],
        compiler_params=pltpu.CompilerParams(
            collective_id=1, has_side_effects=True, vmem_limit_bytes=42 * 2**20
        ),
        cost_estimate=pl.CostEstimate(
            flops=20 * flops, bytes_accessed=200 * 2**20, transcendentals=0
        ),
    )(
        x, wide_x, wide_h, n_first, n_second, inv_first, inv_second, sym, hidden,
        conv_first, conv_second, w_head.T, turned,
    )
    logit_mirror = mirror_unpack(arrived, bins, height).astype(jnp.float32)
    logits = (0.5 * (raw_logits + logit_mirror)).astype(jnp.bfloat16)
    inverse_len = 1.0 / length

    def kernel_grad(table):
        part = table[:folded] * inverse_len
        part = jnp.concatenate([part[:, :channels], part[:, channels : 2 * channels]], axis=0)
        part = part.reshape(3, 3, channels, channels).transpose(1, 0, 3, 2)
        return part.reshape(9, channels, channels)

    sum_first, sum_second = sum_first.reshape(-1, 128), sum_second.reshape(-1, 128)
    head = sum_second[folded : folded + bins] * inverse_len
    return (
        logits,
        grad_x.reshape(channels, height, lanes),
        kernel_grad(sum_first),
        kernel_grad(sum_second),
        head[:, :channels],
        head[:, channels],
    )


def solution(mesh):
    placed = (P(None, "col", "row"), P(), P(), P(), P(), P(None, "col", "row"))
    return jax.shard_map(
        on_device,
        mesh=mesh,
        in_specs=placed,
        out_specs=(P(None, "col", "row"), P(None, "col", "row"), P(), P(), P(), P()),
        check_vma=False,
    )
```
